32 devices in a mesh: lat: 4 (over y, x), lon: 8 (over z, core).
Axes of the slice: x: 2, y: 2, z: 4, core: 2. Of those that a mesh axis runs over, the one named last changes fastest.
Arguments:
- height: float32 [768, 3072], P('lat', 'lon'), may hold values from -6 to 6
- flux_lon: float32 [768, 3072], P('lat', 'lon'), may hold values from -4 to 4
- flux_lat: float32 [768, 3072], P('lat', 'lon'), may hold values from -4 to 4
- depth: float32 [768, 3072], P('lat', 'lon'), may hold values from 0.05 to 1
- wet: int32 [768, 3072], P('lat', 'lon'), may hold values 0 or 1
- kernel: float32 [96, 96, 192], P('lat', None, 'lon'), may hold values from -0.5 to 0.5
Outputs:
- height_out: float32 [768, 3072], P('lat', 'lon')
- flux_lon_out: float32 [768, 3072], P('lat', 'lon')
- flux_lat_out: float32 [768, 3072], P('lat', 'lon')
- loading_out: float32 [96, 192], P('lat', 'lon')
The draws below stay inside these ranges and needn't reach their ends.
All inputs are finite; a program needn't handle non-finite values. No bound on the sum of `wet` on one device may be relied on, other than what follows from the above.
Results may differ from the reference program's by a relative error of at most 0.00011.
Values sent between devices are 32-bit elements; how exact they have to be, the bound alone decides.
A program may use at most 128 MiB of HBM per device.

```python
import math
import jax
import jax.numpy as jnp
from jax import lax

STEPS = 2
ROW_RATIO = 8
COL_RATIO = 16
GRID_ROWS = 768
GRID_COLS = 3072
MASS_ROWS = 96
MASS_COLS = 192


def with_ends(drawn, stream_key, least, largest):
    place = [jax.random.randint(jax.random.fold_in(stream_key, axis), (), 0, length) for axis, length in enumerate(drawn.shape)]
    main_axis = drawn.shape.index(max(drawn.shape))
    next_to = place[:main_axis] + [(place[main_axis] + 1) % drawn.shape[main_axis]] + place[main_axis + 1:]
    return drawn.at[tuple(place)].set(least).at[tuple(next_to)].set(largest)


def shard_levels(own_key, dims, cuts, low, largest):
    factor_of, own = 1.0, jax.random.fold_in(own_key, 6)
    for dim, shards_of in cuts:
        heights = jnp.exp(jax.random.uniform(jax.random.fold_in(own, dim), (shards_of,), jnp.float32, low / len(cuts), largest / len(cuts)))
        factor_of = factor_of * jnp.repeat(heights, dims[dim] // shards_of).reshape([-1 if axis == dim else 1 for axis in range(len(dims))])
    return factor_of


def scatter_about(stream_key, shape, scale, reach, pieces=(), held_as=jnp.bfloat16):
    values = jax.random.normal(stream_key, shape, jnp.float32) * scale
    if len(pieces) > 0:
        values = shard_levels(stream_key, shape, pieces, -0.22, 0.18) * values
    return jnp.clip(values, min=-reach, max=reach).astype(held_as)


def setup_inputs(seed: int = 0) -> dict:
    splits = jax.random.split(jax.random.key(seed), 7)
    return {
        "height": scatter_about(splits[0], (GRID_ROWS, GRID_COLS), 1.0, 6.0, ((0, 4), (1, 8)), jnp.float32),
        "flux_lon": scatter_about(splits[1], (GRID_ROWS, GRID_COLS), 0.3, 4.0, ((0, 4), (1, 8)), jnp.float32),
        "flux_lat": scatter_about(splits[2], (GRID_ROWS, GRID_COLS), 0.3, 4.0, ((0, 4), (1, 8)), jnp.float32),
        "depth": jnp.clip(jnp.exp(math.log(1.0) - 2.9957323 * jax.random.uniform(splits[3], (GRID_ROWS, GRID_COLS), jnp.float32) ** shard_levels(splits[3], (GRID_ROWS, GRID_COLS), ((0, 4), (1, 8)), -0.2, 0.2)), 0.05, 1.0),
        "wet": with_ends((jax.random.randint(splits[4], (GRID_ROWS, GRID_COLS), 0, 8) < 7).astype(jnp.int32), jax.random.fold_in(splits[4], 1), 0, 1),
        "kernel": scatter_about(splits[5], (MASS_ROWS, MASS_ROWS, MASS_COLS), (MASS_ROWS * MASS_COLS // (ROW_RATIO * COL_RATIO)) ** -0.5, 0.5, ((0, 4), (2, 8)), jnp.float32),
    }


angle_step = math.pi / (180.0 * 240.0)
courant_lon = 0.3
courant_lat = 0.3


def coslat(position, total):
    return jnp.cos((position - 0.5 * total) * angle_step)


def convolve(kernel, mass):
    spec_mass = jnp.fft.rfft(mass, axis=1)

    def one_row(kernel_row):
        spec_row = jnp.fft.rfft(kernel_row, axis=1)
        summed = jnp.sum(spec_row * spec_mass, axis=0)
        return jnp.fft.irfft(summed, n=MASS_COLS)

    return lax.map(one_row, kernel).astype(mass.dtype)


def reference(height, flux_lon, flux_lat, depth, wet, kernel):
    wetf = wet.astype(jnp.float32)
    rows = jnp.arange(GRID_ROWS).astype(jnp.float32)
    cos_center = coslat(rows + 0.5, GRID_ROWS)[:, None]
    cos_north = coslat(rows + 1.0, GRID_ROWS)[:, None]
    cos_south = coslat(rows, GRID_ROWS)[:, None]
    zero_row = jnp.zeros((1, GRID_COLS), jnp.float32)
    wet_north = jnp.concatenate([wetf[1:], zero_row], 0)
    depth_north = jnp.concatenate([depth[1:], zero_row], 0)
    wet_east = jnp.roll(wetf, -1, axis=1)
    depth_east = jnp.roll(depth, -1, axis=1)
    loading = jnp.zeros((MASS_ROWS, MASS_COLS), jnp.float32)
    for step_index in range(STEPS):
        weighted = height * wetf * cos_center
        mass = weighted.reshape(MASS_ROWS, ROW_RATIO, MASS_COLS, COL_RATIO).mean(axis=(1, 3))
        loading = convolve(kernel, mass)
        zeta = height + jnp.repeat(jnp.repeat(loading, ROW_RATIO, axis=0), COL_RATIO, axis=1)
        zeta_east = jnp.roll(zeta, -1, axis=1)
        flux_lon = wetf * wet_east * (flux_lon - courant_lon / cos_center * (0.5 * (depth + depth_east)) * (zeta_east - zeta))
        zeta_north = jnp.concatenate([zeta[1:], zero_row], 0)
        flux_lat = wetf * wet_north * (flux_lat - courant_lat * (0.5 * (depth + depth_north)) * (zeta_north - zeta))
        lat_below = jnp.concatenate([zero_row, flux_lat[:-1]], 0)
        lon_west = jnp.roll(flux_lon, 1, axis=1)
        height = wetf * (height - courant_lon / cos_center * (flux_lon - lon_west)
                         - courant_lat / cos_center * (cos_north * flux_lat - cos_south * lat_below))
    return height, flux_lon, flux_lat, loading
```

```python
import functools
import math

import jax
import jax.numpy as jnp
from jax import lax
from jax.experimental import pallas as pl
from jax.experimental.pallas import tpu as pltpu
from jax.sharding import PartitionSpec as P

STEPS = 2
ANGLE_STEP = math.pi / (180.0 * 240.0)
COURANT_LON = 0.3
COURANT_LAT = 0.3
MESH = pl.DeviceIdType.MESH
LANES = 128
SUB = 8
F32 = jnp.float32
BF16 = jnp.bfloat16


def up(value, unit):
    return -(-value // unit) * unit


def lane_of(shape):
    return lax.broadcasted_iota(jnp.int32, shape, len(shape) - 1)


def sub_of(shape):
    return lax.broadcasted_iota(jnp.int32, shape, len(shape) - 2)


def turn(cells, shift, axis):
    shift = shift % cells.shape[axis]
    return cells if shift == 0 else pltpu.roll(cells, shift, axis)


def take(cells, start, width, dest):
    first, offset = start // LANES, start % LANES
    head = turn(cells[:, first * LANES : (first + 1) * LANES], dest - offset, 1)
    if offset + width <= LANES:
        return head
    tail = turn(cells[:, (first + 1) * LANES : (first + 2) * LANES], dest - offset, 1)
    return jnp.where(lane_of(head.shape) < dest + LANES - offset, head, tail)


def halves(cells):
    high = cells.astype(BF16)
    return high, (cells - high.astype(F32)).astype(BF16)


def exact_dot(cells, picks):
    high = cells.astype(BF16).astype(F32)
    rest = cells - high
    middle = rest.astype(BF16).astype(F32)
    terms = jnp.concatenate([high, middle, rest - middle], 0).astype(BF16)
    summed = jnp.dot(terms, picks, preferred_element_type=F32)
    rows = cells.shape[0]
    return summed[:rows] + (summed[rows : 2 * rows] + summed[2 * rows :])


def run(
    lat_n, lon_n,
    height, flux_lon, flux_lat, depth, wet, kernel,
    out_height, out_lon, out_lat, out_loading,
    field, wet_in, kin, state, final, coef, rowc, zeta, gather_m, expand_m,
    kt, khi, klo, mslot, mass_all, psend, precv,
    lonh_send, lonh_recv, lath_send, lath_recv,
    in_sem, out_sem, mass_ss, mass_rs, all_ss, all_rs, part_ss, part_rs,
    kh_ss, kh_rs, lonh_ss, lonh_rs, lath_ss, lath_rs,
):
    lat, lon = lax.axis_index("lat"), lax.axis_index("lon")
    rows, cols = height.shape
    crows, ccols, jrows = kernel.shape
    all_rows, all_cols = field.shape[1:]
    tiles = all_rows // SUB
    jpad = up(jrows, LANES)
    width = mass_all.shape[2]
    north, south = lax.rem(lat + 1, lat_n), lax.rem(lat + lat_n - 1, lat_n)
    east, west = lax.rem(lon + 1, lon_n), lax.rem(lon + lon_n - 1, lon_n)
    lon_peer = [lax.rem(lon + off, lon_n) for off in range(lon_n)]
    lat_peer = [lax.rem(lat + off, lat_n) for off in range(lat_n)]

    def send(src, dst, ss, rs, to):
        copy = pltpu.make_async_remote_copy(
            src_ref=src, dst_ref=dst, send_sem=ss, recv_sem=rs, device_id=to, device_id_type=MESH
        )
        copy.start()
        return copy

    own = (pl.ds(0, rows), pl.ds(0, cols))
    loads = [
        pltpu.make_async_copy(height, field.at[(0, *own)], in_sem.at[0]),
        pltpu.make_async_copy(wet, wet_in, in_sem.at[4]),
        pltpu.make_async_copy(flux_lon, field.at[(1, *own)], in_sem.at[1]),
        pltpu.make_async_copy(flux_lat, field.at[(2, *own)], in_sem.at[2]),
        pltpu.make_async_copy(depth, field.at[(3, *own)], in_sem.at[3]),
        pltpu.make_async_copy(kernel, kin.at[pl.ds(0, crows)], in_sem.at[5]),
    ]
    for copy in loads:
        copy.start()
    barrier = pltpu.get_barrier_semaphore()
    for off in range(1, lon_n):
        pl.semaphore_signal(barrier, inc=1, device_id=(lat, lon_peer[off]), device_id_type=MESH)
    for off in range(1, lat_n):
        pl.semaphore_signal(barrier, inc=1, device_id=(lat_peer[off], lon), device_id_type=MESH)

    place = sub_of((all_rows, LANES))
    place = jnp.where(place >= all_rows - SUB // 2, place - all_rows, place) + lat * rows
    place = place.astype(F32)

    def coslat(position):
        return jnp.cos((position - 0.5 * (rows * lat_n)) * ANGLE_STEP)

    cos_center = coslat(place + 0.5)
    rowc[0] = cos_center
    rowc[1] = COURANT_LON / cos_center
    rowc[2] = COURANT_LAT / cos_center * coslat(place + 1.0)
    rowc[3] = COURANT_LAT / cos_center * coslat(place)
    row_ratio, col_ratio = rows // crows, cols // ccols
    gather_m[...] = jnp.where(
        lax.broadcasted_iota(jnp.int32, (cols, LANES), 0) // col_ratio == lane_of((cols, LANES)),
        1.0 / (row_ratio * col_ratio),
        0.0,
    ).astype(BF16)
    fine = lane_of((LANES, all_cols))
    fine = jnp.where(fine < cols + LANES // 2, 1 + fine // col_ratio, 0)
    expand_m[...] = jnp.where(sub_of((LANES, all_cols)) == fine, 1.0, 0.0).astype(BF16)

    def wide(cells, count):
        return jnp.concatenate([cells] * count, 1)

    def send_mass(step, level):
        weighted = level * field[4, :rows, :cols] * wide(rowc[0, :rows], cols // LANES)
        summed = weighted.reshape(crows, row_ratio, cols).sum(axis=1)
        mass = exact_dot(summed, gather_m[...])
        lanes = lane_of((SUB, LANES))
        packed = mass[:SUB]
        for part in range(1, crows // SUB):
            moved = turn(mass[part * SUB : (part + 1) * SUB], 32 * part, 1)
            packed = jnp.where(lanes >= 32 * part, moved, packed)
        mslot[step, lon] = packed
        if step == 0:
            pl.semaphore_wait(barrier, lon_n + lat_n - 2)
        return [
            send(
                mslot.at[step, lon], mslot.at[step, lon],
                mass_ss.at[step, off], mass_rs.at[step, off], (lat, lon_peer[off]),
            )
            for off in range(1, lon_n)
        ]

    def send_band(step, copies):
        for copy in copies:
            copy.wait_recv()
        lanes = lane_of((SUB, LANES))
        bands = []
        for part in range(crows // SUB):
            pieces = [jnp.zeros((SUB, LANES), F32) for _ in range(width // LANES)]
            for block in range(-(-width // ccols)):
                first = ccols * block
                slot = mslot[step, (block - 1) % lon_n]
                moved = turn(slot, first - 32 * part, 1)
                low, begin = first // LANES, first % LANES
                pieces[low] = jnp.where(lanes >= begin, moved, pieces[low])
                if begin + ccols > LANES and low + 1 < width // LANES:
                    pieces[low + 1] = moved
            bands.append(jnp.concatenate(pieces, 1))
        here = pl.ds(pl.multiple_of(lat * crows, SUB), crows)
        mass_all[step, here] = jnp.concatenate(bands, 0)
        return [
            send(
                mass_all.at[step, here], mass_all.at[step, here],
                all_ss.at[step, off], all_rs.at[step, off], (lat_peer[off], lon),
            )
            for off in range(1, lat_n)
        ]

    def send_partials(step, copies):
        for copy in copies:
            copy.wait_recv()
        mass = mass_all[step]
        both = [mass, turn(mass, ccols // 2, 1)]
        if jpad > jrows:
            blank = jnp.zeros((jpad - jrows, width), F32)
            both = [both[0], blank, both[1], blank]
        high, low = halves(jnp.concatenate(both, 0))
        left = khi[...]
        product = (
            jnp.dot(left, high, preferred_element_type=F32)
            + jnp.dot(klo[...], high, preferred_element_type=F32)
            + jnp.dot(left, low, preferred_element_type=F32)
        )
        lags, shift = ccols // 2, 1
        product = product.reshape(lags, 32, width)
        while lags % 2 == 0:
            product = product.reshape(lags // 2, 2, 32, width)
            lags //= 2
            moved = turn(product[:, 1].reshape(lags * 32, width), shift, 1)
            product = product[:, 0] + moved.reshape(lags, 32, width)
            shift *= 2
        total = product[0]
        for lag in range(1, lags):
            total = total + turn(product[lag], shift * lag, 1)
        lanes = lane_of((SUB, LANES))
        sent = []
        for off in range(lon_n):
            packed = None
            for part in range(4):
                got = take(
                    total[part * SUB : (part + 1) * SUB], ccols * (off + 1) - 1, ccols + 2, 32 * part
                )
                packed = got if part == 0 else jnp.where(lanes >= 32 * part, got, packed)
            if off == 0:
                precv[step, 0] = packed
            else:
                psend[step, off] = packed
                sent.append(
                    send(
                        psend.at[step, off], precv.at[step, off],
                        part_ss.at[step, off], part_rs.at[step, off], (lat, lon_peer[off]),
                    )
                )
        return sent

    def loading_of(step, copies):
        for copy in copies:
            copy.wait_recv()
        total = precv[step, 0]
        for off in range(1, lon_n):
            total = total + precv[step, off]
        return jnp.concatenate([turn(total, -32 * part, 1) for part in range(4)], 0)

    def set_zeta(level, loading):
        spread = exact_dot(loading, expand_m[...])
        sub = sub_of((SUB, all_cols))
        for tile in range(tiles):
            rise = jnp.broadcast_to(spread[tile : tile + 1], (SUB, all_cols))
            if tile == tiles - 1:
                below = jnp.broadcast_to(spread[tile + 1 : tile + 2], (SUB, all_cols))
                rise = jnp.where(sub < SUB // 2, rise, below)
            at = pl.ds(tile * SUB, SUB)
            zeta[at, :] = level[at, :] + rise

    def advance(level, old_lon, old_lat, new):
        sub = sub_of((SUB, all_cols))

        def one(turn_index, below):
            here = lax.rem(turn_index + tiles - 1, tiles)
            after = lax.rem(turn_index, tiles)
            at = pl.ds(pl.multiple_of(here * SUB, SUB), SUB)
            up_at = pl.ds(pl.multiple_of(after * SUB, SUB), SUB)
            z = zeta[at, :]
            z_north = turn(jnp.where(sub == 0, zeta[up_at, :], z), SUB - 1, 0)
            z_east = turn(z, all_cols - 1, 1)
            lon_new = coef[1, at, :] * old_lon[at, :] - coef[0, at, :] * (z_east - z)
            lat_new = coef[3, at, :] * old_lat[at, :] - coef[2, at, :] * (z_north - z)
            lat_south = turn(jnp.where(sub == SUB - 1, below, lat_new), 1, 0)
            count = all_cols // LANES
            new[1, at, :] = lon_new
            new[2, at, :] = lat_new
            new[0, at, :] = field[4, at, :] * (
                level[at, :]
                - wide(rowc[1, at, :], count) * (lon_new - turn(lon_new, 1, 1))
                - (
                    wide(rowc[2, at, :], count) * lat_new
                    - wide(rowc[3, at, :], count) * lat_south
                )
            )
            return lat_new

        lax.fori_loop(0, tiles + 1, one, jnp.zeros((SUB, all_cols), F32))

    loads[0].wait()
    loads[1].wait()
    field[4, :rows, :cols] = wet_in[...].astype(F32)
    mass_copies = send_mass(0, field[0, :rows, :cols])
    pending = list(mass_copies)

    for copy in loads[2:5]:
        copy.wait()
    lanes = lane_of((rows, LANES))
    edges = jnp.zeros((rows, LANES), F32)
    for index in range(5):
        right = turn(field[index, :rows, cols - LANES : cols], 2 + 2 * index, 1)
        left = turn(field[index, :rows, :LANES], 16 + 2 * index, 1)
        edges = jnp.where(lanes // 2 == index, right, edges)
        edges = jnp.where(lanes // 2 == 8 + index, left, edges)
    square = lonh_send.shape[2]
    edges = jnp.concatenate([edges, jnp.zeros((square - rows, LANES), F32)], 0).T
    lonh_send[0] = edges[:16]
    lonh_send[1] = edges[16:32]
    lonh_copies = [
        send(lonh_send.at[0], lonh_recv.at[0], lonh_ss.at[0], lonh_rs.at[0], (lat, east)),
        send(lonh_send.at[1], lonh_recv.at[1], lonh_ss.at[1], lonh_rs.at[1], (lat, west)),
    ]
    pending += lonh_copies

    loads[5].wait()
    kh_copies = [
        send(kin.at[0], kin.at[crows], kh_ss.at[0], kh_rs.at[0], (south, lon)),
        send(kin.at[crows - 1], kin.at[crows + 1], kh_ss.at[1], kh_rs.at[1], (north, lon)),
    ]
    pending += kh_copies
    kt[...] = jnp.zeros(kt.shape, F32)

    band_copies = send_band(0, mass_copies)
    pending += band_copies

    half = ccols // 2
    for copy in kh_copies:
        copy.wait_recv()

    def one_row(row, carry):
        cells = kin[row]
        if jpad > jrows:
            cells = jnp.concatenate([cells, jnp.zeros((ccols, jpad - jrows), F32)], 1)
        for part in range(2):
            for chunk in range(jpad // LANES):
                piece = cells[part * half : (part + 1) * half, chunk * LANES : (chunk + 1) * LANES]
                kt[part * (jpad // LANES) + chunk, pl.ds(row, half, stride=32), :] = piece
        return carry

    lax.fori_loop(0, crows + 2, one_row, 0)
    for chunk in range(kt.shape[0]):
        high, low = halves(kt[chunk])
        khi[:, chunk * LANES : (chunk + 1) * LANES] = high
        klo[:, chunk * LANES : (chunk + 1) * LANES] = low

    part_copies = send_partials(0, band_copies)
    pending += part_copies

    for copy in lonh_copies:
        copy.wait_recv()
    arrived = jnp.concatenate(
        [lonh_recv[0], lonh_recv[1], jnp.zeros((LANES - 32, square), F32)], 0
    ).T[:rows]
    for index in range(5):
        from_west = turn(arrived, LANES - 2 - 2 * index, 1)
        from_east = turn(arrived, -16 - 2 * index, 1)
        field[index, :rows, cols:] = jnp.where(lanes < LANES // 2, from_east, from_west)
    sub = sub_of((SUB, all_cols))
    for side in range(2):
        packs = [jnp.zeros((SUB, all_cols), F32), jnp.zeros((SUB, all_cols), F32)]
        for index in range(5):
            if side == 0:
                edge = turn(field[index, rows - SUB : rows, :], 2 + 2 * index, 0)
            else:
                edge = turn(field[index, :SUB, :], 2 * index, 0)
            packs[index // 4] = jnp.where(sub // 2 == index % 4, edge, packs[index // 4])
        lath_send[side] = jnp.concatenate(packs, 0)
    lath_copies = [
        send(lath_send.at[0], lath_recv.at[0], lath_ss.at[0], lath_rs.at[0], (north, lon)),
        send(lath_send.at[1], lath_recv.at[1], lath_ss.at[1], lath_rs.at[1], (south, lon)),
    ]
    pending += lath_copies
    for copy in lath_copies:
        copy.wait_recv()
    for index in range(5):
        part = pl.ds(SUB * (index // 4), SUB)
        from_south = turn(lath_recv[0, part, :], 6 - 2 * index, 0)
        from_north = turn(lath_recv[1, part, :], -2 * index, 0)
        if index == 4:
            from_south = jnp.where(lat == 0, 0.0, 1.0) * from_south
            from_north = jnp.where(lat == lat_n - 1, 0.0, 1.0) * from_north
        field[index, rows:, :] = jnp.where(sub < SUB // 2, from_north, from_south)

    def factors(here, carry):
        after = lax.rem(here + 1, tiles)
        at = pl.ds(pl.multiple_of(here * SUB, SUB), SUB)
        up_at = pl.ds(pl.multiple_of(after * SUB, SUB), SUB)
        deep, sea = field[3, at, :], field[4, at, :]
        deep_north = turn(jnp.where(sub == 0, field[3, up_at, :], deep), SUB - 1, 0)
        sea_north = turn(jnp.where(sub == 0, field[4, up_at, :], sea), SUB - 1, 0)
        both = sea * turn(sea, all_cols - 1, 1)
        coef[1, at, :] = both
        coef[0, at, :] = (
            both
            * wide(rowc[1, at, :], all_cols // LANES)
            * (0.5 * (deep + turn(deep, all_cols - 1, 1)))
        )
        both = sea * sea_north
        coef[3, at, :] = both
        coef[2, at, :] = both * (COURANT_LAT * 0.5) * (deep + deep_north)
        return carry

    lax.fori_loop(0, tiles, factors, 0)

    set_zeta(field.at[0], loading_of(0, part_copies))
    advance(field.at[0], field.at[1], field.at[2], state)

    mass_copies = send_mass(1, state[0, :rows, :cols])
    band_copies = send_band(1, mass_copies)
    part_copies = send_partials(1, band_copies)
    pending += mass_copies + band_copies + part_copies
    loading = loading_of(1, part_copies)
    set_zeta(state.at[0], loading)
    advance(state.at[0], state.at[1], state.at[2], final)
    results = [
        pltpu.make_async_copy(final.at[(index, *own)], out, out_sem.at[index])
        for index, out in enumerate((out_height, out_lon, out_lat))
    ]
    for copy in results:
        copy.start()
    out_loading[...] = turn(loading[:crows], -1, 1)[:, :ccols]
    for copy in pending:
        copy.wait_send()
    for copy in results:
        copy.wait()


def body(height, flux_lon, flux_lat, depth, wet, kernel):
    lat_n, lon_n = lax.axis_size("lat"), lax.axis_size("lon")
    rows, cols = height.shape
    kernel = kernel.transpose(0, 2, 1)
    crows, ccols, jrows = kernel.shape
    all_rows, all_cols = rows + SUB, cols + LANES
    jpad = up(jrows, LANES)
    width = up(ccols * lon_n + ccols + 1, LANES)
    square = up(rows, LANES)
    lags = 32 * ccols // 2
    dma = pltpu.SemaphoreType.DMA
    block = jax.ShapeDtypeStruct((rows, cols), F32)
    anywhere = pl.BlockSpec(memory_space=pl.ANY)
    return pl.pallas_call(
        functools.partial(run, lat_n, lon_n),
        out_shape=[block, block, block, jax.ShapeDtypeStruct((crows, ccols), F32)],
        in_specs=[anywhere] * 6,
        out_specs=[anywhere] * 3 + [pl.BlockSpec(memory_space=pltpu.VMEM)],
        scratch_shapes=[
            pltpu.VMEM((5, all_rows, all_cols), F32),
            pltpu.VMEM((rows, cols), jnp.int32),
            pltpu.VMEM((crows + 2, ccols, jrows), F32),
            pltpu.VMEM((3, all_rows, all_cols), F32),
            pltpu.VMEM((3, all_rows, all_cols), F32),
            pltpu.VMEM((4, all_rows, all_cols), F32),
            pltpu.VMEM((4, all_rows, LANES), F32),
            pltpu.VMEM((all_rows, all_cols), F32),
            pltpu.VMEM((cols, LANES), BF16),
            pltpu.VMEM((LANES, all_cols), BF16),
            pltpu.VMEM((2 * jpad // LANES, lags, LANES), F32),
            pltpu.VMEM((lags, 2 * jpad), BF16),
            pltpu.VMEM((lags, 2 * jpad), BF16),
            pltpu.VMEM((STEPS, lon_n, SUB, LANES), F32),
            pltpu.VMEM((STEPS, jrows, width), F32),
            pltpu.VMEM((STEPS, lon_n, SUB, LANES), F32),
            pltpu.VMEM((STEPS, lon_n, SUB, LANES), F32),
            pltpu.VMEM((2, 16, square), F32),
            pltpu.VMEM((2, 16, square), F32),
            pltpu.VMEM((2, 16, all_cols), F32),
            pltpu.VMEM((2, 16, all_cols), F32),
            dma((6,)),
            dma((3,)),
            dma((STEPS, lon_n)),
            dma((STEPS, lon_n)),
            dma((STEPS, lat_n)),
            dma((STEPS, lat_n)),
            dma((STEPS, lon_n)),
            dma((STEPS, lon_n)),
            dma((2,)),
            dma((2,)),
            dma((2,)),
            dma((2,)),
            dma((2,)),
            dma((2,)),
        ],
        compiler_params=pltpu.CompilerParams(
            collective_id=0, has_side_effects=True, vmem_limit_bytes=40 * 2**20
        ),
    )(height, flux_lon, flux_lat, depth, wet, kernel)


def solution(mesh):
    return jax.shard_map(
        body,
        mesh=mesh,
        in_specs=(P("lat", "lon"),) * 5 + (P("lat", None, "lon"),),
        out_specs=(P("lat", "lon"),) * 4,
        check_vma=False,
    )
```

```python
import functools
import math

import jax
import jax.numpy as jnp
from jax import lax
from jax.experimental import pallas as pl
from jax.experimental.pallas import tpu as pltpu
from jax.sharding import PartitionSpec as P

STEPS = 2
ANGLE_STEP = math.pi / (180.0 * 240.0)
COURANT_LON = 0.3
COURANT_LAT = 0.3
MESH = pl.DeviceIdType.MESH
LANES = 128
SUB = 8
F32 = jnp.float32
BF16 = jnp.bfloat16


def up(value, unit):
    return -(-value // unit) * unit


def lane_of(shape):
    return lax.broadcasted_iota(jnp.int32, shape, len(shape) - 1)


def sub_of(shape):
    return lax.broadcasted_iota(jnp.int32, shape, len(shape) - 2)


def turn(cells, shift, axis):
    shift = shift % cells.shape[axis]
    return cells if shift == 0 else pltpu.roll(cells, shift, axis)


def take(cells, start, width, dest):
    first, offset = start // LANES, start % LANES
    head = turn(cells[:, first * LANES : (first + 1) * LANES], dest - offset, 1)
    if offset + width <= LANES:
        return head
    tail = turn(cells[:, (first + 1) * LANES : (first + 2) * LANES], dest - offset, 1)
    return jnp.where(lane_of(head.shape) < dest + LANES - offset, head, tail)


def halves(cells):
    high = cells.astype(BF16)
    return high, (cells - high.astype(F32)).astype(BF16)


def exact_dot(cells, picks):
    high = cells.astype(BF16).astype(F32)
    rest = cells - high
    middle = rest.astype(BF16).astype(F32)
    terms = jnp.concatenate([high, middle, rest - middle], 0).astype(BF16)
    summed = jnp.dot(terms, picks, preferred_element_type=F32)
    rows = cells.shape[0]
    return summed[:rows] + (summed[rows : 2 * rows] + summed[2 * rows :])


def run(
    lat_n, lon_n,
    height, flux_lon, flux_lat, depth, wet, kernel,
    out_height, out_lon, out_lat, out_loading,
    field, wet_in, kin, state, final, coef, rowc, ahead, gather_m, expand_m,
    kt, khi, klo, mslot, mass_all, psend, precv,
    lonh_send, lonh_recv, lath_send, lath_recv,
    in_sem, out_sem, mass_ss, mass_rs, all_ss, all_rs, part_ss, part_rs,
    kh_ss, kh_rs, lonh_ss, lonh_rs, lath_ss, lath_rs,
):
    lat, lon = lax.axis_index("lat"), lax.axis_index("lon")
    rows, cols = height.shape
    crows, ccols, jrows = kernel.shape
    all_rows, all_cols = field.shape[1:]
    tiles = all_rows // SUB
    jpad = up(jrows, LANES)
    width = mass_all.shape[2]
    north, south = lax.rem(lat + 1, lat_n), lax.rem(lat + lat_n - 1, lat_n)
    east, west = lax.rem(lon + 1, lon_n), lax.rem(lon + lon_n - 1, lon_n)
    lon_peer = [lax.rem(lon + off, lon_n) for off in range(lon_n)]
    lat_peer = [lax.rem(lat + off, lat_n) for off in range(lat_n)]

    def send(src, dst, ss, rs, to):
        copy = pltpu.make_async_remote_copy(
            src_ref=src, dst_ref=dst, send_sem=ss, recv_sem=rs, device_id=to, device_id_type=MESH
        )
        copy.start()
        return copy

    own = (pl.ds(0, rows), pl.ds(0, cols))
    loads = [
        pltpu.make_async_copy(height, field.at[(0, *own)], in_sem.at[0]),
        pltpu.make_async_copy(wet, wet_in, in_sem.at[4]),
        pltpu.make_async_copy(flux_lon, field.at[(1, *own)], in_sem.at[1]),
        pltpu.make_async_copy(flux_lat, field.at[(2, *own)], in_sem.at[2]),
        pltpu.make_async_copy(depth, field.at[(3, *own)], in_sem.at[3]),
        pltpu.make_async_copy(kernel, kin.at[pl.ds(0, crows)], in_sem.at[5]),
    ]
    for copy in loads:
        copy.start()
    barrier = pltpu.get_barrier_semaphore()
    for off in range(1, lon_n):
        pl.semaphore_signal(barrier, inc=1, device_id=(lat, lon_peer[off]), device_id_type=MESH)
    for off in range(1, lat_n):
        pl.semaphore_signal(barrier, inc=1, device_id=(lat_peer[off], lon), device_id_type=MESH)

    place = sub_of((all_rows, LANES))
    place = jnp.where(place >= all_rows - SUB // 2, place - all_rows, place) + lat * rows
    place = place.astype(F32)

    def coslat(position):
        return jnp.cos((position - 0.5 * (rows * lat_n)) * ANGLE_STEP)

    cos_center = coslat(place + 0.5)
    rowc[0] = cos_center
    row_ratio, col_ratio = rows // crows, cols // ccols
    gather_m[...] = jnp.where(
        lax.broadcasted_iota(jnp.int32, (cols, LANES), 0) // col_ratio == lane_of((cols, LANES)),
        1.0 / (row_ratio * col_ratio),
        0.0,
    ).astype(BF16)
    def wide(cells, count):
        return jnp.concatenate([cells] * count, 1)

    def send_mass(step, level):
        weighted = level * field[4, :rows, :cols] * wide(rowc[0, :rows], cols // LANES)
        summed = weighted.reshape(crows, row_ratio, cols).sum(axis=1)
        mass = exact_dot(summed, gather_m[...])
        lanes = lane_of((SUB, LANES))
        packed = mass[:SUB]
        for part in range(1, crows // SUB):
            moved = turn(mass[part * SUB : (part + 1) * SUB], 32 * part, 1)
            packed = jnp.where(lanes >= 32 * part, moved, packed)
        mslot[step, lon] = packed
        if step == 0:
            pl.semaphore_wait(barrier, lon_n + lat_n - 2)
        return [
            send(
                mslot.at[step, lon], mslot.at[step, lon],
                mass_ss.at[step, off], mass_rs.at[step, off], (lat, lon_peer[off]),
            )
            for off in range(1, lon_n)
        ]

    def send_band(step, copies):
        for copy in copies:
            copy.wait_recv()
        lanes = lane_of((SUB, LANES))
        bands = []
        for part in range(crows // SUB):
            pieces = [jnp.zeros((SUB, LANES), F32) for _ in range(width // LANES)]
            for block in range(-(-width // ccols)):
                first = ccols * block
                slot = mslot[step, (block - 1) % lon_n]
                moved = turn(slot, first - 32 * part, 1)
                low, begin = first // LANES, first % LANES
                pieces[low] = jnp.where(lanes >= begin, moved, pieces[low])
                if begin + ccols > LANES and low + 1 < width // LANES:
                    pieces[low + 1] = moved
            bands.append(jnp.concatenate(pieces, 1))
        here = pl.ds(pl.multiple_of(lat * crows, SUB), crows)
        mass_all[step, here] = jnp.concatenate(bands, 0)
        return [
            send(
                mass_all.at[step, here], mass_all.at[step, here],
                all_ss.at[step, off], all_rs.at[step, off], (lat_peer[off], lon),
            )
            for off in range(1, lat_n)
        ]

    def send_partials(step, copies):
        for copy in copies:
            copy.wait_recv()
        mass = mass_all[step]
        both = [mass, turn(mass, ccols // 2, 1)]
        if jpad > jrows:
            blank = jnp.zeros((jpad - jrows, width), F32)
            both = [both[0], blank, both[1], blank]
        high, low = halves(jnp.concatenate(both, 0))
        left = khi[...]
        product = (
            jnp.dot(left, high, preferred_element_type=F32)
            + jnp.dot(klo[...], high, preferred_element_type=F32)
            + jnp.dot(left, low, preferred_element_type=F32)
        )
        lags, shift = ccols // 2, 1
        product = product.reshape(lags, 32, width)
        while lags % 2 == 0:
            product = product.reshape(lags // 2, 2, 32, width)
            lags //= 2
            moved = turn(product[:, 1].reshape(lags * 32, width), shift, 1)
            product = product[:, 0] + moved.reshape(lags, 32, width)
            shift *= 2
        total = product[0]
        for lag in range(1, lags):
            total = total + turn(product[lag], shift * lag, 1)
        lanes = lane_of((SUB, LANES))
        sent = []
        for off in range(lon_n):
            packed = None
            for part in range(4):
                got = take(
                    total[part * SUB : (part + 1) * SUB], ccols * (off + 1) - 1, ccols + 2, 32 * part
                )
                packed = got if part == 0 else jnp.where(lanes >= 32 * part, got, packed)
            if off == 0:
                precv[step, 0] = packed
            else:
                psend[step, off] = packed
                sent.append(
                    send(
                        psend.at[step, off], precv.at[step, off],
                        part_ss.at[step, off], part_rs.at[step, off], (lat, lon_peer[off]),
                    )
                )
        return sent

    def loading_of(step, copies):
        for copy in copies:
            copy.wait_recv()
        total = precv[step, 0]
        for off in range(1, lon_n):
            total = total + precv[step, off]
        return jnp.concatenate([turn(total, -32 * part, 1) for part in range(4)], 0)

    def prepare(level, old_lon, old_lat):
        sub = sub_of((SUB, all_cols))
        for here in range(tiles):
            at = pl.ds(here * SUB, SUB)
            cells = level[at, :]
            after = level[pl.ds((here + 1) % tiles * SUB, SUB), :]
            rise_east = turn(cells, all_cols - 1, 1) - cells
            rise_north = turn(jnp.where(sub == 0, after, cells), SUB - 1, 0) - cells
            ahead[0, at, :] = coef[1, at, :] * old_lon[at, :] - coef[0, at, :] * rise_east
            ahead[1, at, :] = coef[3, at, :] * old_lat[at, :] - coef[2, at, :] * rise_north

    def spread(loading):
        following = turn(loading, loading.shape[0] - 1, 0)
        first = jnp.broadcast_to(loading[:1], loading.shape)
        north_rise = jnp.where(sub_of(loading.shape) < crows, following - loading, first - following)
        return exact_dot(loading, expand_m[1]), exact_dot(north_rise, expand_m[0])

    def advance(level, loading, new, last):
        sub = sub_of((SUB, all_cols))
        east_rise, north_rise = spread(loading)
        count = all_cols // LANES

        def lat_of(tile):
            at = pl.ds(tile * SUB, SUB)
            rise = jnp.broadcast_to(north_rise[tile : tile + 1], (SUB, all_cols))
            return ahead[1, at, :] - coef[2, at, :] * jnp.where(sub == SUB - 1, rise, 0.0)

        below = lat_of(tiles - 1)
        done = []
        for tile in range(tiles - 1 if last else tiles):
            at = pl.ds(tile * SUB, SUB)
            rise = jnp.broadcast_to(east_rise[tile : tile + 1], (SUB, all_cols))
            if tile == tiles - 1:
                south_rise = jnp.broadcast_to(east_rise[tile + 1 : tile + 2], (SUB, all_cols))
                rise = jnp.where(sub < SUB // 2, rise, south_rise)
            lon_new = ahead[0, at, :] - coef[0, at, :] * rise
            lat_new = lat_of(tile)
            lat_south = turn(jnp.where(sub == SUB - 1, below, lat_new), 1, 0)
            below = lat_new
            new[1, at, :] = lon_new
            new[2, at, :] = lat_new
            new[0, at, :] = field[4, at, :] * (
                level[at, :]
                - wide(rowc[1, at, :], count) * (lon_new - turn(lon_new, 1, 1))
                - (
                    wide(rowc[2, at, :], count) * lat_new
                    - wide(rowc[3, at, :], count) * lat_south
                )
            )
            group = (tiles - 1) // 3
            if last and tile % group == group - 1:
                part = pl.ds((tile + 1 - group) * SUB, group * SUB)
                for index, out in enumerate((out_height, out_lon, out_lat)):
                    copy = pltpu.make_async_copy(
                        new.at[index, part, pl.ds(0, cols)],
                        out.at[part],
                        out_sem.at[index, tile // group],
                    )
                    copy.start()
                    done.append(copy)
        return done

    loads[0].wait()
    loads[1].wait()
    field[4, :rows, :cols] = wet_in[...].astype(F32)
    mass_copies = send_mass(0, field[0, :rows, :cols])
    pending = list(mass_copies)

    for copy in loads[2:5]:
        copy.wait()
    lanes = lane_of((rows, LANES))
    edges = jnp.zeros((rows, LANES), F32)
    for index in range(5):
        right = turn(field[index, :rows, cols - LANES : cols], 2 + 2 * index, 1)
        left = turn(field[index, :rows, :LANES], 16 + 2 * index, 1)
        edges = jnp.where(lanes // 2 == index, right, edges)
        edges = jnp.where(lanes // 2 == 8 + index, left, edges)
    square = lonh_send.shape[2]
    edges = jnp.concatenate([edges, jnp.zeros((square - rows, LANES), F32)], 0).T
    lonh_send[0] = edges[:16]
    lonh_send[1] = edges[16:32]
    lonh_copies = [
        send(lonh_send.at[0], lonh_recv.at[0], lonh_ss.at[0], lonh_rs.at[0], (lat, east)),
        send(lonh_send.at[1], lonh_recv.at[1], lonh_ss.at[1], lonh_rs.at[1], (lat, west)),
    ]
    pending += lonh_copies

    loads[5].wait()
    kh_copies = [
        send(kin.at[0], kin.at[crows], kh_ss.at[0], kh_rs.at[0], (south, lon)),
        send(kin.at[crows - 1], kin.at[crows + 1], kh_ss.at[1], kh_rs.at[1], (north, lon)),
    ]
    pending += kh_copies
    kt[...] = jnp.zeros(kt.shape, F32)

    half = ccols // 2

    def put(row):
        cells = kin[row]
        if jpad > jrows:
            cells = jnp.concatenate([cells, jnp.zeros((ccols, jpad - jrows), F32)], 1)
        for part in range(2):
            for chunk in range(jpad // LANES):
                piece = cells[part * half : (part + 1) * half, chunk * LANES : (chunk + 1) * LANES]
                kt[part * (jpad // LANES) + chunk, pl.ds(row, half, stride=32), :] = piece

    for row in range(crows):
        put(row)

    band_copies = send_band(0, mass_copies)
    pending += band_copies

    for copy in kh_copies:
        copy.wait_recv()
    put(crows)
    put(crows + 1)
    for chunk in range(kt.shape[0]):
        high, low = halves(kt[chunk])
        khi[:, chunk * LANES : (chunk + 1) * LANES] = high
        klo[:, chunk * LANES : (chunk + 1) * LANES] = low


    for copy in lonh_copies:
        copy.wait_recv()
    arrived = jnp.concatenate(
        [lonh_recv[0], lonh_recv[1], jnp.zeros((LANES - 32, square), F32)], 0
    ).T[:rows]
    for index in range(5):
        from_west = turn(arrived, LANES - 2 - 2 * index, 1)
        from_east = turn(arrived, -16 - 2 * index, 1)
        field[index, :rows, cols:] = jnp.where(lanes < LANES // 2, from_east, from_west)
    sub = sub_of((SUB, all_cols))
    for side in range(2):
        packs = [jnp.zeros((SUB, all_cols), F32), jnp.zeros((SUB, all_cols), F32)]
        for index in range(5):
            if side == 0:
                edge = turn(field[index, rows - SUB : rows, :], 2 + 2 * index, 0)
            else:
                edge = turn(field[index, :SUB, :], 2 * index, 0)
            packs[index // 4] = jnp.where(sub // 2 == index % 4, edge, packs[index // 4])
        lath_send[side] = jnp.concatenate(packs, 0)
    lath_copies = [
        send(lath_send.at[0], lath_recv.at[0], lath_ss.at[0], lath_rs.at[0], (north, lon)),
        send(lath_send.at[1], lath_recv.at[1], lath_ss.at[1], lath_rs.at[1], (south, lon)),
    ]
    pending += lath_copies

    cos_center = rowc[0]
    rowc[1] = COURANT_LON / cos_center
    rowc[2] = COURANT_LAT / cos_center * coslat(place + 1.0)
    rowc[3] = COURANT_LAT / cos_center * coslat(place)
    fine = lane_of((LANES, all_cols))

    def coarse(column):
        return jnp.where(column < cols + LANES // 2, 1 + column // col_ratio, 0)

    own_cell = sub_of((LANES, all_cols)) == coarse(fine)
    next_fine = jnp.where(fine == all_cols - 1, 0, fine + 1)
    east_cell = sub_of((LANES, all_cols)) == coarse(next_fine)
    own_cell, east_cell = jnp.where(own_cell, 1.0, 0.0), jnp.where(east_cell, 1.0, 0.0)
    expand_m[0] = own_cell.astype(BF16)
    expand_m[1] = (east_cell - own_cell).astype(BF16)

    part_copies = send_partials(0, band_copies)
    pending += part_copies

    for copy in lath_copies:
        copy.wait_recv()
    for index in range(5):
        part = pl.ds(SUB * (index // 4), SUB)
        from_south = turn(lath_recv[0, part, :], 6 - 2 * index, 0)
        from_north = turn(lath_recv[1, part, :], -2 * index, 0)
        if index == 4:
            from_south = jnp.where(lat == 0, 0.0, 1.0) * from_south
            from_north = jnp.where(lat == lat_n - 1, 0.0, 1.0) * from_north
        field[index, rows:, :] = jnp.where(sub < SUB // 2, from_north, from_south)

    for here in range(tiles):
        at = pl.ds(here * SUB, SUB)
        up_at = pl.ds((here + 1) % tiles * SUB, SUB)
        deep, sea = field[3, at, :], field[4, at, :]
        deep_north = turn(jnp.where(sub == 0, field[3, up_at, :], deep), SUB - 1, 0)
        sea_north = turn(jnp.where(sub == 0, field[4, up_at, :], sea), SUB - 1, 0)
        both = sea * turn(sea, all_cols - 1, 1)
        coef[1, at, :] = both
        coef[0, at, :] = (
            both
            * wide(rowc[1, at, :], all_cols // LANES)
            * (0.5 * (deep + turn(deep, all_cols - 1, 1)))
        )
        both = sea * sea_north
        coef[3, at, :] = both
        coef[2, at, :] = both * (COURANT_LAT * 0.5) * (deep + deep_north)
    prepare(field.at[0], field.at[1], field.at[2])

    advance(field.at[0], loading_of(0, part_copies), state, False)

    mass_copies = send_mass(1, state[0, :rows, :cols])
    prepare(state.at[0], state.at[1], state.at[2])
    band_copies = send_band(1, mass_copies)
    part_copies = send_partials(1, band_copies)
    pending += mass_copies + band_copies + part_copies
    loading = loading_of(1, part_copies)
    out_loading[...] = turn(loading[:crows], -1, 1)[:, :ccols]
    results = advance(state.at[0], loading, final, True)
    for copy in pending:
        copy.wait_send()
    for copy in results:
        copy.wait()


def body(height, flux_lon, flux_lat, depth, wet, kernel):
    lat_n, lon_n = lax.axis_size("lat"), lax.axis_size("lon")
    rows, cols = height.shape
    kernel = kernel.transpose(0, 2, 1)
    crows, ccols, jrows = kernel.shape
    all_rows, all_cols = rows + SUB, cols + LANES
    jpad = up(jrows, LANES)
    width = up(ccols * lon_n + ccols + 1, LANES)
    square = up(rows, LANES)
    lags = 32 * ccols // 2
    dma = pltpu.SemaphoreType.DMA
    block = jax.ShapeDtypeStruct((rows, cols), F32)
    anywhere = pl.BlockSpec(memory_space=pl.ANY)
    return pl.pallas_call(
        functools.partial(run, lat_n, lon_n),
        out_shape=[block, block, block, jax.ShapeDtypeStruct((crows, ccols), F32)],
        in_specs=[anywhere] * 6,
        out_specs=[anywhere] * 3 + [pl.BlockSpec(memory_space=pltpu.VMEM)],
        scratch_shapes=[
            pltpu.VMEM((5, all_rows, all_cols), F32),
            pltpu.VMEM((rows, cols), jnp.int32),
            pltpu.VMEM((crows + 2, ccols, jrows), F32),
            pltpu.VMEM((3, all_rows, all_cols), F32),
            pltpu.VMEM((3, all_rows, all_cols), F32),
            pltpu.VMEM((4, all_rows, all_cols), F32),
            pltpu.VMEM((4, all_rows, LANES), F32),
            pltpu.VMEM((2, all_rows, all_cols), F32),
            pltpu.VMEM((cols, LANES), BF16),
            pltpu.VMEM((2, LANES, all_cols), BF16),
            pltpu.VMEM((2 * jpad // LANES, lags, LANES), F32),
            pltpu.VMEM((lags, 2 * jpad), BF16),
            pltpu.VMEM((lags, 2 * jpad), BF16),
            pltpu.VMEM((STEPS, lon_n, SUB, LANES), F32),
            pltpu.VMEM((STEPS, jrows, width), F32),
            pltpu.VMEM((STEPS, lon_n, SUB, LANES), F32),
            pltpu.VMEM((STEPS, lon_n, SUB, LANES), F32),
            pltpu.VMEM((2, 16, square), F32),
            pltpu.VMEM((2, 16, square), F32),
            pltpu.VMEM((2, 16, all_cols), F32),
            pltpu.VMEM((2, 16, all_cols), F32),
            dma((6,)),
            dma((3, 3)),
            dma((STEPS, lon_n)),
            dma((STEPS, lon_n)),
            dma((STEPS, lat_n)),
            dma((STEPS, lat_n)),
            dma((STEPS, lon_n)),
            dma((STEPS, lon_n)),
            dma((2,)),
            dma((2,)),
            dma((2,)),
            dma((2,)),
            dma((2,)),
            dma((2,)),
        ],
        compiler_params=pltpu.CompilerParams(
            collective_id=0, has_side_effects=True, vmem_limit_bytes=64 * 2**20
        ),
    )(height, flux_lon, flux_lat, depth, wet, kernel)


def solution(mesh):
    return jax.shard_map(
        body,
        mesh=mesh,
        in_specs=(P("lat", "lon"),) * 5 + (P("lat", None, "lon"),),
        out_specs=(P("lat", "lon"),) * 4,
        check_vma=False,
    )
```

```python
import functools
import math

import jax
import jax.numpy as jnp
from jax import lax
from jax.experimental import pallas as pl
from jax.experimental.pallas import tpu as pltpu
from jax.sharding import PartitionSpec as P

STEPS = 2
ANGLE_STEP = math.pi / (180.0 * 240.0)
COURANT_LON = 0.3
COURANT_LAT = 0.3
MESH = pl.DeviceIdType.MESH
LANES = 128
SUB = 8
F32 = jnp.float32
BF16 = jnp.bfloat16


def up(value, unit):
    return -(-value // unit) * unit


def lane_of(shape):
    return lax.broadcasted_iota(jnp.int32, shape, len(shape) - 1)


def sub_of(shape):
    return lax.broadcasted_iota(jnp.int32, shape, len(shape) - 2)


def turn(cells, shift, axis):
    shift = shift % cells.shape[axis]
    return cells if shift == 0 else pltpu.roll(cells, shift, axis)


def take(cells, start, width, dest):
    first, offset = start // LANES, start % LANES
    head = turn(cells[:, first * LANES : (first + 1) * LANES], dest - offset, 1)
    if offset + width <= LANES:
        return head
    tail = turn(cells[:, (first + 1) * LANES : (first + 2) * LANES], dest - offset, 1)
    return jnp.where(lane_of(head.shape) < dest + LANES - offset, head, tail)


def halves(cells):
    high = cells.astype(BF16)
    return high, (cells - high.astype(F32)).astype(BF16)


def exact_dot(cells, picks):
    high = cells.astype(BF16).astype(F32)
    rest = cells - high
    middle = rest.astype(BF16).astype(F32)
    terms = jnp.concatenate([high, middle, rest - middle], 0).astype(BF16)
    summed = jnp.dot(terms, picks, preferred_element_type=F32)
    rows = cells.shape[0]
    return summed[:rows] + (summed[rows : 2 * rows] + summed[2 * rows :])


def run(
    lat_n, lon_n,
    height, flux_lon, flux_lat, depth, wet, kernel,
    out_height, out_lon, out_lat, out_loading,
    field, wet_in, kin, state, final, coef, rowc, ahead, gather_m, expand_m,
    kt, khi, klo, mslot, mass_all, psend, precv,
    lonh_send, lonh_recv, lath_send, lath_recv,
    in_sem, out_sem, mass_ss, mass_rs, all_ss, all_rs, part_ss, part_rs,
    kh_ss, kh_rs, lonh_ss, lonh_rs, lath_ss, lath_rs,
):
    lat, lon = lax.axis_index("lat"), lax.axis_index("lon")
    rows, cols = height.shape
    crows, ccols, jrows = kernel.shape
    all_rows, all_cols = field.shape[1:]
    tiles = all_rows // SUB
    jpad = up(jrows, LANES)
    width = mass_all.shape[2]
    north, south = lax.rem(lat + 1, lat_n), lax.rem(lat + lat_n - 1, lat_n)
    east, west = lax.rem(lon + 1, lon_n), lax.rem(lon + lon_n - 1, lon_n)
    lon_peer = [lax.rem(lon + off, lon_n) for off in range(lon_n)]
    lat_peer = [lax.rem(lat + off, lat_n) for off in range(lat_n)]

    def send(src, dst, ss, rs, to):
        copy = pltpu.make_async_remote_copy(
            src_ref=src, dst_ref=dst, send_sem=ss, recv_sem=rs, device_id=to, device_id_type=MESH
        )
        copy.start()
        return copy

    own = (pl.ds(0, rows), pl.ds(0, cols))
    loads = [
        pltpu.make_async_copy(height, field.at[(0, *own)], in_sem.at[0]),
        pltpu.make_async_copy(wet, wet_in, in_sem.at[4]),
        pltpu.make_async_copy(flux_lon, field.at[(1, *own)], in_sem.at[1]),
        pltpu.make_async_copy(flux_lat, field.at[(2, *own)], in_sem.at[2]),
        pltpu.make_async_copy(depth, field.at[(3, *own)], in_sem.at[3]),
        pltpu.make_async_copy(kernel, kin.at[pl.ds(0, crows)], in_sem.at[5]),
    ]
    for copy in loads:
        copy.start()
    barrier = pltpu.get_barrier_semaphore()
    for off in range(1, lon_n):
        pl.semaphore_signal(barrier, inc=1, device_id=(lat, lon_peer[off]), device_id_type=MESH)
    for off in range(1, lat_n):
        pl.semaphore_signal(barrier, inc=1, device_id=(lat_peer[off], lon), device_id_type=MESH)

    place = sub_of((all_rows, LANES))
    place = jnp.where(place >= all_rows - SUB // 2, place - all_rows, place) + lat * rows
    place = place.astype(F32)

    def coslat(position):
        return jnp.cos((position - 0.5 * (rows * lat_n)) * ANGLE_STEP)

    cos_center = coslat(place + 0.5)
    rowc[0] = cos_center
    row_ratio, col_ratio = rows // crows, cols // ccols
    gather_m[...] = jnp.where(
        lax.broadcasted_iota(jnp.int32, (cols, LANES), 0) // col_ratio == lane_of((cols, LANES)),
        1.0 / (row_ratio * col_ratio),
        0.0,
    ).astype(BF16)
    rowc[1] = COURANT_LON / cos_center
    rowc[2] = COURANT_LAT / cos_center * coslat(place + 1.0)
    rowc[3] = COURANT_LAT / cos_center * coslat(place)
    fine = lane_of((LANES, all_cols))

    def coarse(column):
        return jnp.where(column < cols + LANES // 2, 1 + column // col_ratio, 0)

    own_cell = sub_of((LANES, all_cols)) == coarse(fine)
    next_fine = jnp.where(fine == all_cols - 1, 0, fine + 1)
    east_cell = sub_of((LANES, all_cols)) == coarse(next_fine)
    own_cell, east_cell = jnp.where(own_cell, 1.0, 0.0), jnp.where(east_cell, 1.0, 0.0)
    expand_m[0] = own_cell.astype(BF16)
    expand_m[1] = (east_cell - own_cell).astype(BF16)

    def wide(cells, count):
        return jnp.concatenate([cells] * count, 1)

    def send_mass(step, level):
        weighted = level * field[4, :rows, :cols] * wide(rowc[0, :rows], cols // LANES)
        summed = weighted.reshape(crows, row_ratio, cols).sum(axis=1)
        mass = exact_dot(summed, gather_m[...])
        lanes = lane_of((SUB, LANES))
        packed = mass[:SUB]
        for part in range(1, crows // SUB):
            moved = turn(mass[part * SUB : (part + 1) * SUB], 32 * part, 1)
            packed = jnp.where(lanes >= 32 * part, moved, packed)
        mslot[step, lon] = packed
        if step == 0:
            pl.semaphore_wait(barrier, lon_n + lat_n - 2)
        return [
            send(
                mslot.at[step, lon], mslot.at[step, lon],
                mass_ss.at[step, off], mass_rs.at[step, off], (lat, lon_peer[off]),
            )
            for off in range(1, lon_n)
        ]

    def send_band(step, copies):
        for copy in copies:
            copy.wait_recv()
        lanes = lane_of((SUB, LANES))
        bands = []
        for part in range(crows // SUB):
            pieces = [jnp.zeros((SUB, LANES), F32) for _ in range(width // LANES)]
            for block in range(-(-width // ccols)):
                first = ccols * block
                slot = mslot[step, (block - 1) % lon_n]
                moved = turn(slot, first - 32 * part, 1)
                low, begin = first // LANES, first % LANES
                pieces[low] = jnp.where(lanes >= begin, moved, pieces[low])
                if begin + ccols > LANES and low + 1 < width // LANES:
                    pieces[low + 1] = moved
            bands.append(jnp.concatenate(pieces, 1))
        here = pl.ds(pl.multiple_of(lat * crows, SUB), crows)
        mass_all[step, here] = jnp.concatenate(bands, 0)
        return [
            send(
                mass_all.at[step, here], mass_all.at[step, here],
                all_ss.at[step, off], all_rs.at[step, off], (lat_peer[off], lon),
            )
            for off in range(1, lat_n)
        ]

    def send_partials(step, copies):
        for copy in copies:
            copy.wait_recv()
        mass = mass_all[step]
        both = [mass, turn(mass, ccols // 2, 1)]
        if jpad > jrows:
            blank = jnp.zeros((jpad - jrows, width), F32)
            both = [both[0], blank, both[1], blank]
        high, low = halves(jnp.concatenate(both, 0))
        left = khi[...]
        product = (
            jnp.dot(left, high, preferred_element_type=F32)
            + jnp.dot(klo[...], high, preferred_element_type=F32)
            + jnp.dot(left, low, preferred_element_type=F32)
        )
        lags, shift = ccols // 2, 1
        product = product.reshape(lags, 32, width)
        while lags % 2 == 0:
            product = product.reshape(lags // 2, 2, 32, width)
            lags //= 2
            moved = turn(product[:, 1].reshape(lags * 32, width), shift, 1)
            product = product[:, 0] + moved.reshape(lags, 32, width)
            shift *= 2
        total = product[0]
        for lag in range(1, lags):
            total = total + turn(product[lag], shift * lag, 1)
        lanes = lane_of((SUB, LANES))
        sent = []
        for off in range(lon_n):
            packed = None
            for part in range(4):
                got = take(
                    total[part * SUB : (part + 1) * SUB], ccols * (off + 1) - 1, ccols + 2, 32 * part
                )
                packed = got if part == 0 else jnp.where(lanes >= 32 * part, got, packed)
            if off == 0:
                precv[step, 0] = packed
            else:
                psend[step, off] = packed
                sent.append(
                    send(
                        psend.at[step, off], precv.at[step, off],
                        part_ss.at[step, off], part_rs.at[step, off], (lat, lon_peer[off]),
                    )
                )
        return sent

    def loading_of(step, copies):
        for copy in copies:
            copy.wait_recv()
        total = precv[step, 0]
        for off in range(1, lon_n):
            total = total + precv[step, off]
        return jnp.concatenate([turn(total, -32 * part, 1) for part in range(4)], 0)

    def prepare(level, old_lon, old_lat):
        sub = sub_of((SUB, all_cols))
        for here in range(tiles):
            at = pl.ds(here * SUB, SUB)
            cells = level[at, :]
            after = level[pl.ds((here + 1) % tiles * SUB, SUB), :]
            rise_east = turn(cells, all_cols - 1, 1) - cells
            rise_north = turn(jnp.where(sub == 0, after, cells), SUB - 1, 0) - cells
            ahead[0, at, :] = coef[1, at, :] * old_lon[at, :] - coef[0, at, :] * rise_east
            ahead[1, at, :] = coef[3, at, :] * old_lat[at, :] - coef[2, at, :] * rise_north

    def spread(loading):
        following = turn(loading, loading.shape[0] - 1, 0)
        first = jnp.broadcast_to(loading[:1], loading.shape)
        north_rise = jnp.where(sub_of(loading.shape) < crows, following - loading, first - following)
        return exact_dot(loading, expand_m[1]), exact_dot(north_rise, expand_m[0])

    def advance(level, loading, new, last):
        sub = sub_of((SUB, all_cols))
        east_rise, north_rise = spread(loading)
        count = all_cols // LANES

        def lat_of(tile):
            at = pl.ds(tile * SUB, SUB)
            rise = jnp.broadcast_to(north_rise[tile : tile + 1], (SUB, all_cols))
            return ahead[1, at, :] - coef[2, at, :] * jnp.where(sub == SUB - 1, rise, 0.0)

        below = lat_of(tiles - 1)
        done = []
        for tile in range(tiles - 1 if last else tiles):
            at = pl.ds(tile * SUB, SUB)
            rise = jnp.broadcast_to(east_rise[tile : tile + 1], (SUB, all_cols))
            if tile == tiles - 1:
                south_rise = jnp.broadcast_to(east_rise[tile + 1 : tile + 2], (SUB, all_cols))
                rise = jnp.where(sub < SUB // 2, rise, south_rise)
            lon_new = ahead[0, at, :] - coef[0, at, :] * rise
            lat_new = lat_of(tile)
            lat_south = turn(jnp.where(sub == SUB - 1, below, lat_new), 1, 0)
            below = lat_new
            new[1, at, :] = lon_new
            new[2, at, :] = lat_new
            new[0, at, :] = field[4, at, :] * (
                level[at, :]
                - wide(rowc[1, at, :], count) * (lon_new - turn(lon_new, 1, 1))
                - (
                    wide(rowc[2, at, :], count) * lat_new
                    - wide(rowc[3, at, :], count) * lat_south
                )
            )
            group = (tiles - 1) // 3
            if last and tile % group == group - 1:
                part = pl.ds((tile + 1 - group) * SUB, group * SUB)
                for index, out in enumerate((out_height, out_lon, out_lat)):
                    copy = pltpu.make_async_copy(
                        new.at[index, part, pl.ds(0, cols)],
                        out.at[part],
                        out_sem.at[index, tile // group],
                    )
                    copy.start()
                    done.append(copy)
        return done

    loads[0].wait()
    loads[1].wait()
    field[4, :rows, :cols] = wet_in[...].astype(F32)
    mass_copies = send_mass(0, field[0, :rows, :cols])
    pending = list(mass_copies)

    for copy in loads[2:5]:
        copy.wait()
    lanes = lane_of((rows, LANES))
    edges = jnp.zeros((rows, LANES), F32)
    for index in range(5):
        right = turn(field[index, :rows, cols - LANES : cols], 2 + 2 * index, 1)
        left = turn(field[index, :rows, :LANES], 16 + 2 * index, 1)
        edges = jnp.where(lanes // 2 == index, right, edges)
        edges = jnp.where(lanes // 2 == 8 + index, left, edges)
    square = lonh_send.shape[2]
    edges = jnp.concatenate([edges, jnp.zeros((square - rows, LANES), F32)], 0).T
    lonh_send[0] = edges[:16]
    lonh_send[1] = edges[16:32]
    lonh_copies = [
        send(lonh_send.at[0], lonh_recv.at[0], lonh_ss.at[0], lonh_rs.at[0], (lat, east)),
        send(lonh_send.at[1], lonh_recv.at[1], lonh_ss.at[1], lonh_rs.at[1], (lat, west)),
    ]
    pending += lonh_copies

    loads[5].wait()
    kh_copies = [
        send(kin.at[0], kin.at[crows], kh_ss.at[0], kh_rs.at[0], (south, lon)),
        send(kin.at[crows - 1], kin.at[crows + 1], kh_ss.at[1], kh_rs.at[1], (north, lon)),
    ]
    pending += kh_copies
    kt[...] = jnp.zeros(kt.shape, F32)

    half = ccols // 2

    def put(row):
        cells = kin[row]
        if jpad > jrows:
            cells = jnp.concatenate([cells, jnp.zeros((ccols, jpad - jrows), F32)], 1)
        for part in range(2):
            for chunk in range(jpad // LANES):
                piece = cells[part * half : (part + 1) * half, chunk * LANES : (chunk + 1) * LANES]
                kt[part * (jpad // LANES) + chunk, pl.ds(row, half, stride=32), :] = piece

    for row in range(crows):
        put(row)

    band_copies = send_band(0, mass_copies)
    pending += band_copies

    for copy in kh_copies:
        copy.wait_recv()
    put(crows)
    put(crows + 1)
    for chunk in range(kt.shape[0]):
        high, low = halves(kt[chunk])
        khi[:, chunk * LANES : (chunk + 1) * LANES] = high
        klo[:, chunk * LANES : (chunk + 1) * LANES] = low


    for copy in lonh_copies:
        copy.wait_recv()
    arrived = jnp.concatenate(
        [lonh_recv[0], lonh_recv[1], jnp.zeros((LANES - 32, square), F32)], 0
    ).T[:rows]
    for index in range(5):
        from_west = turn(arrived, LANES - 2 - 2 * index, 1)
        from_east = turn(arrived, -16 - 2 * index, 1)
        field[index, :rows, cols:] = jnp.where(lanes < LANES // 2, from_east, from_west)
    sub = sub_of((SUB, all_cols))
    for side in range(2):
        packs = [jnp.zeros((SUB, all_cols), F32), jnp.zeros((SUB, all_cols), F32)]
        for index in range(5):
            if side == 0:
                edge = turn(field[index, rows - SUB : rows, :], 2 + 2 * index, 0)
            else:
                edge = turn(field[index, :SUB, :], 2 * index, 0)
            packs[index // 4] = jnp.where(sub // 2 == index % 4, edge, packs[index // 4])
        lath_send[side] = jnp.concatenate(packs, 0)
    lath_copies = [
        send(lath_send.at[0], lath_recv.at[0], lath_ss.at[0], lath_rs.at[0], (north, lon)),
        send(lath_send.at[1], lath_recv.at[1], lath_ss.at[1], lath_rs.at[1], (south, lon)),
    ]
    pending += lath_copies

    part_copies = send_partials(0, band_copies)
    pending += part_copies

    for copy in lath_copies:
        copy.wait_recv()
    for index in range(5):
        part = pl.ds(SUB * (index // 4), SUB)
        from_south = turn(lath_recv[0, part, :], 6 - 2 * index, 0)
        from_north = turn(lath_recv[1, part, :], -2 * index, 0)
        if index == 4:
            from_south = jnp.where(lat == 0, 0.0, 1.0) * from_south
            from_north = jnp.where(lat == lat_n - 1, 0.0, 1.0) * from_north
        field[index, rows:, :] = jnp.where(sub < SUB // 2, from_north, from_south)

    for here in range(tiles):
        at = pl.ds(here * SUB, SUB)
        up_at = pl.ds((here + 1) % tiles * SUB, SUB)
        deep, sea = field[3, at, :], field[4, at, :]
        deep_north = turn(jnp.where(sub == 0, field[3, up_at, :], deep), SUB - 1, 0)
        sea_north = turn(jnp.where(sub == 0, field[4, up_at, :], sea), SUB - 1, 0)
        both = sea * turn(sea, all_cols - 1, 1)
        coef[1, at, :] = both
        coef[0, at, :] = (
            both
            * wide(rowc[1, at, :], all_cols // LANES)
            * (0.5 * (deep + turn(deep, all_cols - 1, 1)))
        )
        both = sea * sea_north
        coef[3, at, :] = both
        coef[2, at, :] = both * (COURANT_LAT * 0.5) * (deep + deep_north)
    prepare(field.at[0], field.at[1], field.at[2])

    advance(field.at[0], loading_of(0, part_copies), state, False)

    mass_copies = send_mass(1, state[0, :rows, :cols])
    prepare(state.at[0], state.at[1], state.at[2])
    band_copies = send_band(1, mass_copies)
    part_copies = send_partials(1, band_copies)
    pending += mass_copies + band_copies + part_copies
    loading = loading_of(1, part_copies)
    out_loading[...] = turn(loading[:crows], -1, 1)[:, :ccols]
    results = advance(state.at[0], loading, final, True)
    for copy in pending:
        copy.wait_send()
    for copy in results:
        copy.wait()


def hand_over(*refs):
    sems = refs[-1]
    count = len(refs) // 2
    copies = [
        pltpu.make_async_copy(refs[index], refs[count + index], sems.at[index])
        for index in range(count)
    ]
    for copy in copies:
        copy.start()
    for copy in copies:
        copy.wait()


def body(height, flux_lon, flux_lat, depth, wet, kernel):
    lat_n, lon_n = lax.axis_size("lat"), lax.axis_size("lon")
    rows, cols = height.shape
    kernel = kernel.transpose(0, 2, 1)
    crows, ccols, jrows = kernel.shape
    all_rows, all_cols = rows + SUB, cols + LANES
    jpad = up(jrows, LANES)
    width = up(ccols * lon_n + ccols + 1, LANES)
    square = up(rows, LANES)
    lags = 32 * ccols // 2
    dma = pltpu.SemaphoreType.DMA
    block = jax.ShapeDtypeStruct((rows, cols), F32)
    anywhere = pl.BlockSpec(memory_space=pl.ANY)
    results = pl.pallas_call(
        functools.partial(run, lat_n, lon_n),
        out_shape=[block, block, block, jax.ShapeDtypeStruct((crows, ccols), F32)],
        in_specs=[anywhere] * 6,
        out_specs=[anywhere] * 3 + [pl.BlockSpec(memory_space=pltpu.VMEM)],
        scratch_shapes=[
            pltpu.VMEM((5, all_rows, all_cols), F32),
            pltpu.VMEM((rows, cols), jnp.int32),
            pltpu.VMEM((crows + 2, ccols, jrows), F32),
            pltpu.VMEM((3, all_rows, all_cols), F32),
            pltpu.VMEM((3, all_rows, all_cols), F32),
            pltpu.VMEM((4, all_rows, all_cols), F32),
            pltpu.VMEM((4, all_rows, LANES), F32),
            pltpu.VMEM((2, all_rows, all_cols), F32),
            pltpu.VMEM((cols, LANES), BF16),
            pltpu.VMEM((2, LANES, all_cols), BF16),
            pltpu.VMEM((2 * jpad // LANES, lags, LANES), F32),
            pltpu.VMEM((lags, 2 * jpad), BF16),
            pltpu.VMEM((lags, 2 * jpad), BF16),
            pltpu.VMEM((STEPS, lon_n, SUB, LANES), F32),
            pltpu.VMEM((STEPS, jrows, width), F32),
            pltpu.VMEM((STEPS, lon_n, SUB, LANES), F32),
            pltpu.VMEM((STEPS, lon_n, SUB, LANES), F32),
            pltpu.VMEM((2, 16, square), F32),
            pltpu.VMEM((2, 16, square), F32),
            pltpu.VMEM((2, 16, all_cols), F32),
            pltpu.VMEM((2, 16, all_cols), F32),
            dma((6,)),
            dma((3, 3)),
            dma((STEPS, lon_n)),
            dma((STEPS, lon_n)),
            dma((STEPS, lat_n)),
            dma((STEPS, lat_n)),
            dma((STEPS, lon_n)),
            dma((STEPS, lon_n)),
            dma((2,)),
            dma((2,)),
            dma((2,)),
            dma((2,)),
            dma((2,)),
            dma((2,)),
        ],
        compiler_params=pltpu.CompilerParams(
            collective_id=0, has_side_effects=True, vmem_limit_bytes=64 * 2**20
        ),
    )(height, flux_lon, flux_lat, depth, wet, kernel)
    return pl.pallas_call(
        hand_over,
        out_shape=[jax.ShapeDtypeStruct(result.shape, F32) for result in results],
        in_specs=[anywhere] * 4,
        out_specs=[anywhere] * 4,
        scratch_shapes=[dma((4,))],
        compiler_params=pltpu.CompilerParams(vmem_limit_bytes=64 * 2**20),
    )(*results)


def solution(mesh):
    return jax.shard_map(
        body,
        mesh=mesh,
        in_specs=(P("lat", "lon"),) * 5 + (P("lat", None, "lon"),),
        out_specs=(P("lat", "lon"),) * 4,
        check_vma=False,
    )
```

```python
import functools
import math

import jax
import jax.numpy as jnp
from jax import lax
from jax.experimental import pallas as pl
from jax.experimental.pallas import tpu as pltpu
from jax.sharding import PartitionSpec as P

STEPS = 2
ANGLE_STEP = math.pi / (180.0 * 240.0)
COURANT_LON = 0.3
COURANT_LAT = 0.3
MESH = pl.DeviceIdType.MESH
LANES = 128
SUB = 8
F32 = jnp.float32
BF16 = jnp.bfloat16


def up(value, unit):
    return -(-value // unit) * unit


def lane_of(shape):
    return lax.broadcasted_iota(jnp.int32, shape, len(shape) - 1)


def sub_of(shape):
    return lax.broadcasted_iota(jnp.int32, shape, len(shape) - 2)


def turn(cells, shift, axis):
    shift = shift % cells.shape[axis]
    return cells if shift == 0 else pltpu.roll(cells, shift, axis)


def take(cells, start, width, dest):
    first, offset = start // LANES, start % LANES
    head = turn(cells[:, first * LANES : (first + 1) * LANES], dest - offset, 1)
    if offset + width <= LANES:
        return head
    tail = turn(cells[:, (first + 1) * LANES : (first + 2) * LANES], dest - offset, 1)
    return jnp.where(lane_of(head.shape) < dest + LANES - offset, head, tail)


def halves(cells):
    high = cells.astype(BF16)
    return high, (cells - high.astype(F32)).astype(BF16)


def exact_dot(cells, picks):
    high = cells.astype(BF16).astype(F32)
    rest = cells - high
    middle = rest.astype(BF16).astype(F32)
    terms = jnp.concatenate([high, middle, rest - middle], 0).astype(BF16)
    summed = jnp.dot(terms, picks, preferred_element_type=F32)
    rows = cells.shape[0]
    return summed[:rows] + (summed[rows : 2 * rows] + summed[2 * rows :])


def wide(cells, count):
    return jnp.concatenate([cells] * count, 1)


def expanders(all_cols, cols, col_ratio):
    shape = (LANES, all_cols)
    fine = lane_of(shape)

    def cell(column):
        coarse = jnp.where(column < cols + LANES // 2, 1 + column // col_ratio, 0)
        return jnp.where(sub_of(shape) == coarse, 1.0, 0.0)

    own = cell(fine)
    east = cell(jnp.where(fine == all_cols - 1, 0, fine + 1))
    return own.astype(BF16), (east - own).astype(BF16)


def spread(loading, crows, expand, expand_rise):
    following = turn(loading, loading.shape[0] - 1, 0)
    first = jnp.broadcast_to(loading[:1], loading.shape)
    north_rise = jnp.where(sub_of(loading.shape) < crows, following - loading, first - following)
    return exact_dot(loading, expand_rise), exact_dot(north_rise, expand)


def advance(level, ahead, factor, sea, rowc, rises, new, last, before, after):
    all_rows, all_cols = level.shape
    tiles = all_rows // SUB
    sub = sub_of((SUB, all_cols))
    east_rise, north_rise = rises
    count = all_cols // LANES

    def lat_of(tile):
        at = pl.ds(tile * SUB, SUB)
        rise = jnp.broadcast_to(north_rise[tile : tile + 1], (SUB, all_cols))
        return ahead[1][at, :] - factor[1][at, :] * jnp.where(sub == SUB - 1, rise, 0.0)

    before(tiles - 1)
    below = lat_of(tiles - 1)
    for tile in range(tiles - 1 if last else tiles):
        before(tile)
        at = pl.ds(tile * SUB, SUB)
        rise = jnp.broadcast_to(east_rise[tile : tile + 1], (SUB, all_cols))
        if tile == tiles - 1:
            south_rise = jnp.broadcast_to(east_rise[tile + 1 : tile + 2], (SUB, all_cols))
            rise = jnp.where(sub < SUB // 2, rise, south_rise)
        lon_new = ahead[0][at, :] - factor[0][at, :] * rise
        lat_new = lat_of(tile)
        lat_south = turn(jnp.where(sub == SUB - 1, below, lat_new), 1, 0)
        below = lat_new
        new[1, at, :] = lon_new
        new[2, at, :] = lat_new
        new[0, at, :] = sea[at, :] * (
            level[at, :]
            - wide(rowc[1, at, :], count) * (lon_new - turn(lon_new, 1, 1))
            - (
                wide(rowc[2, at, :], count) * lat_new
                - wide(rowc[3, at, :], count) * lat_south
            )
        )
        after(tile)


GROUPS = 3


def finish(
    pack, rowc_in, loading_in, out_height, out_lon, out_lat, out_loading,
    have, rowc, loading_ref, final, pack_sem, row_sem, load_sem, out_sem,
):
    rows, cols = out_height.shape
    crows, ccols = out_loading.shape
    all_rows, all_cols = have.shape[1:]
    tiles = all_rows // SUB
    group = rows // GROUPS
    get_loading = pltpu.make_async_copy(loading_in, loading_ref, load_sem)
    get_rowc = pltpu.make_async_copy(rowc_in, rowc, row_sem)
    parts = [pl.ds(rows, SUB)] + [pl.ds(index * group, group) for index in range(GROUPS)]
    gets = [
        pltpu.make_async_copy(pack.at[:, part], have.at[:, part], pack_sem.at[index])
        for index, part in enumerate(parts)
    ]
    for copy in [get_loading, get_rowc, *gets]:
        copy.start()
    expand, expand_rise = expanders(all_cols, cols, cols // ccols)
    get_loading.wait()
    loading = loading_ref[...]
    out_loading[...] = turn(loading[:crows], -1, 1)[:, :ccols]
    rises = spread(loading, crows, expand, expand_rise)
    get_rowc.wait()
    puts = []
    per = group // SUB

    def before(tile):
        if tile == tiles - 1:
            gets[0].wait()
        elif tile % per == 0:
            gets[1 + tile // per].wait()

    def after(tile):
        if tile % per == per - 1:
            part = parts[1 + tile // per]
            for index, out in enumerate((out_height, out_lon, out_lat)):
                copy = pltpu.make_async_copy(
                    final.at[index, part, pl.ds(0, cols)],
                    out.at[part],
                    out_sem.at[index, tile // per],
                )
                copy.start()
                puts.append(copy)

    advance(
        have.at[5], (have.at[3], have.at[4]), (have.at[0], have.at[1]), have.at[2], rowc, rises,
        final, True, before, after,
    )
    for copy in puts:
        copy.wait()


def run(
    lat_n, lon_n,
    height, flux_lon, flux_lat, depth, wet, kernel,
    out_pack, out_rowc, out_loading,
    field, wet_in, kin, state, coef, rowc, ahead, gather_m, expand_m,
    kt, khi, klo, mslot, mass_all, psend, precv,
    lonh_send, lonh_recv, lath_send, lath_recv,
    in_sem, out_sem, mass_ss, mass_rs, all_ss, all_rs, part_ss, part_rs,
    kh_ss, kh_rs, lonh_ss, lonh_rs, lath_ss, lath_rs,
):
    lat, lon = lax.axis_index("lat"), lax.axis_index("lon")
    rows, cols = height.shape
    crows, ccols, jrows = kernel.shape
    all_rows, all_cols = field.shape[1:]
    tiles = all_rows // SUB
    jpad = up(jrows, LANES)
    width = mass_all.shape[2]
    north, south = lax.rem(lat + 1, lat_n), lax.rem(lat + lat_n - 1, lat_n)
    east, west = lax.rem(lon + 1, lon_n), lax.rem(lon + lon_n - 1, lon_n)
    lon_peer = [lax.rem(lon + off, lon_n) for off in range(lon_n)]
    lat_peer = [lax.rem(lat + off, lat_n) for off in range(lat_n)]

    def send(src, dst, ss, rs, to):
        copy = pltpu.make_async_remote_copy(
            src_ref=src, dst_ref=dst, send_sem=ss, recv_sem=rs, device_id=to, device_id_type=MESH
        )
        copy.start()
        return copy

    own = (pl.ds(0, rows), pl.ds(0, cols))
    loads = [
        pltpu.make_async_copy(height, field.at[(0, *own)], in_sem.at[0]),
        pltpu.make_async_copy(wet, wet_in, in_sem.at[4]),
        pltpu.make_async_copy(flux_lon, field.at[(1, *own)], in_sem.at[1]),
        pltpu.make_async_copy(flux_lat, field.at[(2, *own)], in_sem.at[2]),
        pltpu.make_async_copy(depth, field.at[(3, *own)], in_sem.at[3]),
        pltpu.make_async_copy(kernel, kin.at[pl.ds(0, crows)], in_sem.at[5]),
    ]
    for copy in loads:
        copy.start()
    barrier = pltpu.get_barrier_semaphore()
    for off in range(1, lon_n):
        pl.semaphore_signal(barrier, inc=1, device_id=(lat, lon_peer[off]), device_id_type=MESH)
    for off in range(1, lat_n):
        pl.semaphore_signal(barrier, inc=1, device_id=(lat_peer[off], lon), device_id_type=MESH)

    place = sub_of((all_rows, LANES))
    place = jnp.where(place >= all_rows - SUB // 2, place - all_rows, place) + lat * rows
    place = place.astype(F32)

    def coslat(position):
        return jnp.cos((position - 0.5 * (rows * lat_n)) * ANGLE_STEP)

    cos_center = coslat(place + 0.5)
    rowc[0] = cos_center
    row_ratio, col_ratio = rows // crows, cols // ccols
    gather_m[...] = jnp.where(
        lax.broadcasted_iota(jnp.int32, (cols, LANES), 0) // col_ratio == lane_of((cols, LANES)),
        1.0 / (row_ratio * col_ratio),
        0.0,
    ).astype(BF16)
    rowc[1] = COURANT_LON / cos_center
    rowc[2] = COURANT_LAT / cos_center * coslat(place + 1.0)
    rowc[3] = COURANT_LAT / cos_center * coslat(place)
    expand_m[0], expand_m[1] = expanders(all_cols, cols, col_ratio)

    def send_mass(step, level):
        weighted = level * field[4, :rows, :cols] * wide(rowc[0, :rows], cols // LANES)
        summed = weighted.reshape(crows, row_ratio, cols).sum(axis=1)
        mass = exact_dot(summed, gather_m[...])
        lanes = lane_of((SUB, LANES))
        packed = mass[:SUB]
        for part in range(1, crows // SUB):
            moved = turn(mass[part * SUB : (part + 1) * SUB], 32 * part, 1)
            packed = jnp.where(lanes >= 32 * part, moved, packed)
        mslot[step, lon] = packed
        if step == 0:
            pl.semaphore_wait(barrier, lon_n + lat_n - 2)
        return [
            send(
                mslot.at[step, lon], mslot.at[step, lon],
                mass_ss.at[step, off], mass_rs.at[step, off], (lat, lon_peer[off]),
            )
            for off in range(1, lon_n)
        ]

    def send_band(step, copies):
        for copy in copies:
            copy.wait_recv()
        lanes = lane_of((SUB, LANES))
        bands = []
        for part in range(crows // SUB):
            pieces = [jnp.zeros((SUB, LANES), F32) for _ in range(width // LANES)]
            for block in range(-(-width // ccols)):
                first = ccols * block
                slot = mslot[step, (block - 1) % lon_n]
                moved = turn(slot, first - 32 * part, 1)
                low, begin = first // LANES, first % LANES
                pieces[low] = jnp.where(lanes >= begin, moved, pieces[low])
                if begin + ccols > LANES and low + 1 < width // LANES:
                    pieces[low + 1] = moved
            bands.append(jnp.concatenate(pieces, 1))
        here = pl.ds(pl.multiple_of(lat * crows, SUB), crows)
        mass_all[step, here] = jnp.concatenate(bands, 0)
        return [
            send(
                mass_all.at[step, here], mass_all.at[step, here],
                all_ss.at[step, off], all_rs.at[step, off], (lat_peer[off], lon),
            )
            for off in range(1, lat_n)
        ]

    def send_partials(step, copies):
        for copy in copies:
            copy.wait_recv()
        mass = mass_all[step]
        both = [mass, turn(mass, ccols // 2, 1)]
        if jpad > jrows:
            blank = jnp.zeros((jpad - jrows, width), F32)
            both = [both[0], blank, both[1], blank]
        high, low = halves(jnp.concatenate(both, 0))
        left = khi[...]
        product = (
            jnp.dot(left, high, preferred_element_type=F32)
            + jnp.dot(klo[...], high, preferred_element_type=F32)
            + jnp.dot(left, low, preferred_element_type=F32)
        )
        lags, shift = ccols // 2, 1
        product = product.reshape(lags, 32, width)
        while lags % 2 == 0:
            product = product.reshape(lags // 2, 2, 32, width)
            lags //= 2
            moved = turn(product[:, 1].reshape(lags * 32, width), shift, 1)
            product = product[:, 0] + moved.reshape(lags, 32, width)
            shift *= 2
        total = product[0]
        for lag in range(1, lags):
            total = total + turn(product[lag], shift * lag, 1)
        lanes = lane_of((SUB, LANES))
        sent = []
        for off in range(lon_n):
            packed = None
            for part in range(4):
                got = take(
                    total[part * SUB : (part + 1) * SUB], ccols * (off + 1) - 1, ccols + 2, 32 * part
                )
                packed = got if part == 0 else jnp.where(lanes >= 32 * part, got, packed)
            if off == 0:
                precv[step, 0] = packed
            else:
                psend[step, off] = packed
                sent.append(
                    send(
                        psend.at[step, off], precv.at[step, off],
                        part_ss.at[step, off], part_rs.at[step, off], (lat, lon_peer[off]),
                    )
                )
        return sent

    def loading_of(step, copies):
        for copy in copies:
            copy.wait_recv()
        total = precv[step, 0]
        for off in range(1, lon_n):
            total = total + precv[step, off]
        return jnp.concatenate([turn(total, -32 * part, 1) for part in range(4)], 0)

    def prepare(step, level, old_lon, old_lat):
        sub = sub_of((SUB, all_cols))
        for here in range(tiles):
            at = pl.ds(here * SUB, SUB)
            cells = level[at, :]
            after = level[pl.ds((here + 1) % tiles * SUB, SUB), :]
            rise_east = turn(cells, all_cols - 1, 1) - cells
            rise_north = turn(jnp.where(sub == 0, after, cells), SUB - 1, 0) - cells
            ahead[step, 0, at, :] = coef[1, at, :] * old_lon[at, :] - coef[0, at, :] * rise_east
            ahead[step, 1, at, :] = coef[3, at, :] * old_lat[at, :] - coef[2, at, :] * rise_north

    loads[0].wait()
    loads[1].wait()
    field[4, :rows, :cols] = wet_in[...].astype(F32)
    mass_copies = send_mass(0, field[0, :rows, :cols])
    pending = list(mass_copies)

    for copy in loads[2:5]:
        copy.wait()
    lanes = lane_of((rows, LANES))
    edges = jnp.zeros((rows, LANES), F32)
    for index in range(5):
        right = turn(field[index, :rows, cols - LANES : cols], 2 + 2 * index, 1)
        left = turn(field[index, :rows, :LANES], 16 + 2 * index, 1)
        edges = jnp.where(lanes // 2 == index, right, edges)
        edges = jnp.where(lanes // 2 == 8 + index, left, edges)
    square = lonh_send.shape[2]
    edges = jnp.concatenate([edges, jnp.zeros((square - rows, LANES), F32)], 0).T
    lonh_send[0] = edges[:16]
    lonh_send[1] = edges[16:32]
    lonh_copies = [
        send(lonh_send.at[0], lonh_recv.at[0], lonh_ss.at[0], lonh_rs.at[0], (lat, east)),
        send(lonh_send.at[1], lonh_recv.at[1], lonh_ss.at[1], lonh_rs.at[1], (lat, west)),
    ]
    pending += lonh_copies

    loads[5].wait()
    kh_copies = [
        send(kin.at[0], kin.at[crows], kh_ss.at[0], kh_rs.at[0], (south, lon)),
        send(kin.at[crows - 1], kin.at[crows + 1], kh_ss.at[1], kh_rs.at[1], (north, lon)),
    ]
    pending += kh_copies
    kt[...] = jnp.zeros(kt.shape, F32)

    half = ccols // 2

    def put(row):
        cells = kin[row]
        if jpad > jrows:
            cells = jnp.concatenate([cells, jnp.zeros((ccols, jpad - jrows), F32)], 1)
        for part in range(2):
            for chunk in range(jpad // LANES):
                piece = cells[part * half : (part + 1) * half, chunk * LANES : (chunk + 1) * LANES]
                kt[part * (jpad // LANES) + chunk, pl.ds(row, half, stride=32), :] = piece

    for row in range(crows):
        put(row)

    band_copies = send_band(0, mass_copies)
    pending += band_copies

    for copy in kh_copies:
        copy.wait_recv()
    put(crows)
    put(crows + 1)
    for chunk in range(kt.shape[0]):
        high, low = halves(kt[chunk])
        khi[:, chunk * LANES : (chunk + 1) * LANES] = high
        klo[:, chunk * LANES : (chunk + 1) * LANES] = low


    for copy in lonh_copies:
        copy.wait_recv()
    arrived = jnp.concatenate(
        [lonh_recv[0], lonh_recv[1], jnp.zeros((LANES - 32, square), F32)], 0
    ).T[:rows]
    for index in range(5):
        from_west = turn(arrived, LANES - 2 - 2 * index, 1)
        from_east = turn(arrived, -16 - 2 * index, 1)
        field[index, :rows, cols:] = jnp.where(lanes < LANES // 2, from_east, from_west)
    sub = sub_of((SUB, all_cols))
    for side in range(2):
        packs = [jnp.zeros((SUB, all_cols), F32), jnp.zeros((SUB, all_cols), F32)]
        for index in range(5):
            if side == 0:
                edge = turn(field[index, rows - SUB : rows, :], 2 + 2 * index, 0)
            else:
                edge = turn(field[index, :SUB, :], 2 * index, 0)
            packs[index // 4] = jnp.where(sub // 2 == index % 4, edge, packs[index // 4])
        lath_send[side] = jnp.concatenate(packs, 0)
    lath_copies = [
        send(lath_send.at[0], lath_recv.at[0], lath_ss.at[0], lath_rs.at[0], (north, lon)),
        send(lath_send.at[1], lath_recv.at[1], lath_ss.at[1], lath_rs.at[1], (south, lon)),
    ]
    pending += lath_copies

    part_copies = send_partials(0, band_copies)
    pending += part_copies

    for copy in lath_copies:
        copy.wait_recv()
    for index in range(5):
        part = pl.ds(SUB * (index // 4), SUB)
        from_south = turn(lath_recv[0, part, :], 6 - 2 * index, 0)
        from_north = turn(lath_recv[1, part, :], -2 * index, 0)
        if index == 4:
            from_south = jnp.where(lat == 0, 0.0, 1.0) * from_south
            from_north = jnp.where(lat == lat_n - 1, 0.0, 1.0) * from_north
        field[index, rows:, :] = jnp.where(sub < SUB // 2, from_north, from_south)

    for here in range(tiles):
        at = pl.ds(here * SUB, SUB)
        up_at = pl.ds((here + 1) % tiles * SUB, SUB)
        deep, sea = field[3, at, :], field[4, at, :]
        deep_north = turn(jnp.where(sub == 0, field[3, up_at, :], deep), SUB - 1, 0)
        sea_north = turn(jnp.where(sub == 0, field[4, up_at, :], sea), SUB - 1, 0)
        both = sea * turn(sea, all_cols - 1, 1)
        coef[1, at, :] = both
        coef[0, at, :] = (
            both
            * wide(rowc[1, at, :], all_cols // LANES)
            * (0.5 * (deep + turn(deep, all_cols - 1, 1)))
        )
        both = sea * sea_north
        coef[3, at, :] = both
        coef[2, at, :] = both * (COURANT_LAT * 0.5) * (deep + deep_north)
    prepare(0, field.at[0], field.at[1], field.at[2])

    results = []

    def keep(*pairs):
        for src, dst in pairs:
            copy = pltpu.make_async_copy(src, dst, out_sem.at[len(results)])
            copy.start()
            results.append(copy)

    keep(
        (rowc, out_rowc),
        (coef.at[0], out_pack.at[0]),
        (coef.at[2], out_pack.at[1]),
        (field.at[4], out_pack.at[2]),
    )
    rises = spread(loading_of(0, part_copies), crows, expand_m[0], expand_m[1])
    advance(
        field.at[0], (ahead.at[0, 0], ahead.at[0, 1]), (coef.at[0], coef.at[2]), field.at[4],
        rowc, rises, state, False, lambda tile: None, lambda tile: None,
    )

    mass_copies = send_mass(1, state[0, :rows, :cols])
    prepare(1, state.at[0], state.at[1], state.at[2])
    keep(
        (ahead.at[1, 0], out_pack.at[3]),
        (ahead.at[1, 1], out_pack.at[4]),
        (state.at[0], out_pack.at[5]),
    )
    band_copies = send_band(1, mass_copies)
    part_copies = send_partials(1, band_copies)
    pending += mass_copies + band_copies + part_copies
    out_loading[...] = loading_of(1, part_copies)
    for copy in pending:
        copy.wait_send()
    for copy in results:
        copy.wait()


def body(height, flux_lon, flux_lat, depth, wet, kernel):
    lat_n, lon_n = lax.axis_size("lat"), lax.axis_size("lon")
    rows, cols = height.shape
    kernel = kernel.transpose(0, 2, 1)
    crows, ccols, jrows = kernel.shape
    all_rows, all_cols = rows + SUB, cols + LANES
    jpad = up(jrows, LANES)
    width = up(ccols * lon_n + ccols + 1, LANES)
    square = up(rows, LANES)
    lags = 32 * ccols // 2
    dma = pltpu.SemaphoreType.DMA
    block = jax.ShapeDtypeStruct((rows, cols), F32)
    inside = pl.BlockSpec(memory_space=pltpu.VMEM)
    pack = jax.ShapeDtypeStruct((6, all_rows, all_cols), F32)
    factors = jax.ShapeDtypeStruct((4, all_rows, LANES), F32)
    anywhere = pl.BlockSpec(memory_space=pl.ANY)
    results = pl.pallas_call(
        functools.partial(run, lat_n, lon_n),
        out_shape=[pack, factors, jax.ShapeDtypeStruct((32, LANES), F32)],
        in_specs=[anywhere] * 6,
        out_specs=[anywhere, anywhere, inside],
        scratch_shapes=[
            pltpu.VMEM((5, all_rows, all_cols), F32),
            pltpu.VMEM((rows, cols), jnp.int32),
            pltpu.VMEM((crows + 2, ccols, jrows), F32),
            pltpu.VMEM((3, all_rows, all_cols), F32),
            pltpu.VMEM((4, all_rows, all_cols), F32),
            pltpu.VMEM((4, all_rows, LANES), F32),
            pltpu.VMEM((STEPS, 2, all_rows, all_cols), F32),
            pltpu.VMEM((cols, LANES), BF16),
            pltpu.VMEM((2, LANES, all_cols), BF16),
            pltpu.VMEM((2 * jpad // LANES, lags, LANES), F32),
            pltpu.VMEM((lags, 2 * jpad), BF16),
            pltpu.VMEM((lags, 2 * jpad), BF16),
            pltpu.VMEM((STEPS, lon_n, SUB, LANES), F32),
            pltpu.VMEM((STEPS, jrows, width), F32),
            pltpu.VMEM((STEPS, lon_n, SUB, LANES), F32),
            pltpu.VMEM((STEPS, lon_n, SUB, LANES), F32),
            pltpu.VMEM((2, 16, square), F32),
            pltpu.VMEM((2, 16, square), F32),
            pltpu.VMEM((2, 16, all_cols), F32),
            pltpu.VMEM((2, 16, all_cols), F32),
            dma((6,)),
            dma((7,)),
            dma((STEPS, lon_n)),
            dma((STEPS, lon_n)),
            dma((STEPS, lat_n)),
            dma((STEPS, lat_n)),
            dma((STEPS, lon_n)),
            dma((STEPS, lon_n)),
            dma((2,)),
            dma((2,)),
            dma((2,)),
            dma((2,)),
            dma((2,)),
            dma((2,)),
        ],
        compiler_params=pltpu.CompilerParams(
            collective_id=0, has_side_effects=True, vmem_limit_bytes=64 * 2**20
        ),
    )(height, flux_lon, flux_lat, depth, wet, kernel)
    return pl.pallas_call(
        finish,
        out_shape=[block, block, block, jax.ShapeDtypeStruct((crows, ccols), F32)],
        in_specs=[anywhere] * 3,
        out_specs=[anywhere] * 3 + [inside],
        scratch_shapes=[
            pltpu.VMEM((6, all_rows, all_cols), F32),
            pltpu.VMEM((4, all_rows, LANES), F32),
            pltpu.VMEM((32, LANES), F32),
            pltpu.VMEM((3, all_rows, all_cols), F32),
            dma((GROUPS + 1,)),
            dma(()),
            dma(()),
            dma((3, GROUPS)),
        ],
        compiler_params=pltpu.CompilerParams(vmem_limit_bytes=64 * 2**20),
    )(*results)


def solution(mesh):
    return jax.shard_map(
        body,
        mesh=mesh,
        in_specs=(P("lat", "lon"),) * 5 + (P("lat", None, "lon"),),
        out_specs=(P("lat", "lon"),) * 4,
        check_vma=False,
    )
```

```python
import functools
import math

import jax
import jax.numpy as jnp
from jax import lax
from jax.experimental import pallas as pl
from jax.experimental.pallas import tpu as pltpu
from jax.sharding import PartitionSpec as P

STEPS = 2
ANGLE_STEP = math.pi / (180.0 * 240.0)
COURANT_LON = 0.3
COURANT_LAT = 0.3
MESH = pl.DeviceIdType.MESH
LANES = 128
SUB = 8
F32 = jnp.float32
BF16 = jnp.bfloat16


def up(value, unit):
    return -(-value // unit) * unit


def lane_of(shape):
    return lax.broadcasted_iota(jnp.int32, shape, len(shape) - 1)


def sub_of(shape):
    return lax.broadcasted_iota(jnp.int32, shape, len(shape) - 2)


def turn(cells, shift, axis):
    shift = shift % cells.shape[axis]
    return cells if shift == 0 else pltpu.roll(cells, shift, axis)


def take(cells, start, width, dest):
    first, offset = start // LANES, start % LANES
    head = turn(cells[:, first * LANES : (first + 1) * LANES], dest - offset, 1)
    if offset + width <= LANES:
        return head
    tail = turn(cells[:, (first + 1) * LANES : (first + 2) * LANES], dest - offset, 1)
    return jnp.where(lane_of(head.shape) < dest + LANES - offset, head, tail)


def halves(cells):
    high = cells.astype(BF16)
    return high, (cells - high.astype(F32)).astype(BF16)


def exact_dot(cells, picks):
    high = cells.astype(BF16).astype(F32)
    rest = cells - high
    middle = rest.astype(BF16).astype(F32)
    terms = jnp.concatenate([high, middle, rest - middle], 0).astype(BF16)
    summed = jnp.dot(terms, picks, preferred_element_type=F32)
    rows = cells.shape[0]
    return summed[:rows] + (summed[rows : 2 * rows] + summed[2 * rows :])


def wide(cells, count):
    return jnp.concatenate([cells] * count, 1)


def expanders(all_cols, cols, col_ratio):
    shape = (LANES, all_cols)
    fine = lane_of(shape)

    def cell(column):
        coarse = jnp.where(column < cols + LANES // 2, 1 + column // col_ratio, 0)
        return jnp.where(sub_of(shape) == coarse, 1.0, 0.0)

    own = cell(fine)
    east = cell(jnp.where(fine == all_cols - 1, 0, fine + 1))
    return own.astype(BF16), (east - own).astype(BF16)


def spread(loading, crows, expand, expand_rise):
    following = turn(loading, loading.shape[0] - 1, 0)
    first = jnp.broadcast_to(loading[:1], loading.shape)
    north_rise = jnp.where(sub_of(loading.shape) < crows, following - loading, first - following)
    return exact_dot(loading, expand_rise), exact_dot(north_rise, expand)


def advance(level, ahead, factor, sea, rowc, rises, new, last, before, after):
    all_rows, all_cols = level.shape
    tiles = all_rows // SUB
    sub = sub_of((SUB, all_cols))
    east_rise, north_rise = rises
    count = all_cols // LANES

    def lat_of(tile):
        at = pl.ds(tile * SUB, SUB)
        rise = jnp.broadcast_to(north_rise[tile : tile + 1], (SUB, all_cols))
        return ahead[1][at, :] - factor[1][at, :] * jnp.where(sub == SUB - 1, rise, 0.0)

    before(tiles - 1)
    below = lat_of(tiles - 1)
    for tile in range(tiles - 1 if last else tiles):
        before(tile)
        at = pl.ds(tile * SUB, SUB)
        rise = jnp.broadcast_to(east_rise[tile : tile + 1], (SUB, all_cols))
        if tile == tiles - 1:
            south_rise = jnp.broadcast_to(east_rise[tile + 1 : tile + 2], (SUB, all_cols))
            rise = jnp.where(sub < SUB // 2, rise, south_rise)
        lon_new = ahead[0][at, :] - factor[0][at, :] * rise
        lat_new = lat_of(tile)
        lat_south = turn(jnp.where(sub == SUB - 1, below, lat_new), 1, 0)
        below = lat_new
        new[1, at, :] = lon_new
        new[2, at, :] = lat_new
        new[0, at, :] = sea[at, :] * (
            level[at, :]
            - wide(rowc[1, at, :], count) * (lon_new - turn(lon_new, 1, 1))
            - (
                wide(rowc[2, at, :], count) * lat_new
                - wide(rowc[3, at, :], count) * lat_south
            )
        )
        after(tile)


GROUPS = 3


def finish(
    pack, rowc_in, loading_in, out_height, out_lon, out_lat, out_loading,
    have, rowc, loading_ref, final, pack_sem, row_sem, load_sem, out_sem,
):
    rows, cols = out_height.shape
    crows, ccols = out_loading.shape
    all_rows, all_cols = have.shape[1:]
    tiles = all_rows // SUB
    group = rows // GROUPS
    get_loading = pltpu.make_async_copy(loading_in, loading_ref, load_sem)
    get_rowc = pltpu.make_async_copy(rowc_in, rowc, row_sem)
    parts = [pl.ds(rows, SUB)] + [pl.ds(index * group, group) for index in range(GROUPS)]
    gets = [
        pltpu.make_async_copy(pack.at[:, part], have.at[:, part], pack_sem.at[index])
        for index, part in enumerate(parts)
    ]
    for copy in [get_loading, get_rowc, *gets]:
        copy.start()
    expand, expand_rise = expanders(all_cols, cols, cols // ccols)
    get_loading.wait()
    loading = loading_ref[...]
    out_loading[...] = turn(loading[:crows], -1, 1)[:, :ccols]
    rises = spread(loading, crows, expand, expand_rise)
    get_rowc.wait()
    puts = []
    per = group // SUB

    def before(tile):
        if tile == tiles - 1:
            gets[0].wait()
        elif tile % per == 0:
            gets[1 + tile // per].wait()

    def after(tile):
        if tile % per == per - 1:
            part = parts[1 + tile // per]
            for index, out in enumerate((out_height, out_lon, out_lat)):
                copy = pltpu.make_async_copy(
                    final.at[index, part, pl.ds(0, cols)],
                    out.at[part],
                    out_sem.at[index, tile // per],
                )
                copy.start()
                puts.append(copy)

    advance(
        have.at[5], (have.at[3], have.at[4]), (have.at[0], have.at[1]), have.at[2], rowc, rises,
        final, True, before, after,
    )
    for copy in puts:
        copy.wait()


def run(
    lat_n, lon_n,
    height, flux_lon, flux_lat, depth, wet, kernel,
    out_pack, out_rowc, out_loading,
    field, wet_in, kin, state, coef, rowc, ahead, gather_m, expand_m,
    kt, khi, klo, mslot, psend, precv,
    lonh_send, lonh_recv, lath_send, lath_recv,
    in_sem, out_sem, mass_ss, mass_rs, all_ss, all_rs, part_ss, part_rs,
    kh_ss, kh_rs, lonh_ss, lonh_rs, lath_ss, lath_rs,
):
    lat, lon = lax.axis_index("lat"), lax.axis_index("lon")
    rows, cols = height.shape
    crows, ccols, jrows = kernel.shape
    all_rows, all_cols = field.shape[1:]
    tiles = all_rows // SUB
    jpad = up(jrows, LANES)
    width = up(ccols * lon_n + ccols + 1, LANES)
    north, south = lax.rem(lat + 1, lat_n), lax.rem(lat + lat_n - 1, lat_n)
    east, west = lax.rem(lon + 1, lon_n), lax.rem(lon + lon_n - 1, lon_n)
    lon_peer = [lax.rem(lon + off, lon_n) for off in range(lon_n)]
    lat_peer = [lax.rem(lat + off, lat_n) for off in range(lat_n)]

    def send(src, dst, ss, rs, to):
        copy = pltpu.make_async_remote_copy(
            src_ref=src, dst_ref=dst, send_sem=ss, recv_sem=rs, device_id=to, device_id_type=MESH
        )
        copy.start()
        return copy

    own = (pl.ds(0, rows), pl.ds(0, cols))
    loads = [
        pltpu.make_async_copy(height, field.at[(0, *own)], in_sem.at[0]),
        pltpu.make_async_copy(wet, wet_in, in_sem.at[4]),
        pltpu.make_async_copy(flux_lon, field.at[(1, *own)], in_sem.at[1]),
        pltpu.make_async_copy(flux_lat, field.at[(2, *own)], in_sem.at[2]),
        pltpu.make_async_copy(depth, field.at[(3, *own)], in_sem.at[3]),
        pltpu.make_async_copy(kernel, kin.at[pl.ds(0, crows)], in_sem.at[5]),
    ]
    for copy in loads:
        copy.start()
    barrier = pltpu.get_barrier_semaphore()
    for off in range(1, lon_n):
        pl.semaphore_signal(barrier, inc=1, device_id=(lat, lon_peer[off]), device_id_type=MESH)
    for off in range(1, lat_n):
        pl.semaphore_signal(barrier, inc=1, device_id=(lat_peer[off], lon), device_id_type=MESH)

    place = sub_of((all_rows, LANES))
    place = jnp.where(place >= all_rows - SUB // 2, place - all_rows, place) + lat * rows
    place = place.astype(F32)

    def coslat(position):
        return jnp.cos((position - 0.5 * (rows * lat_n)) * ANGLE_STEP)

    cos_center = coslat(place + 0.5)
    rowc[0] = cos_center
    row_ratio, col_ratio = rows // crows, cols // ccols
    gather_m[...] = jnp.where(
        lax.broadcasted_iota(jnp.int32, (cols, LANES), 0) // col_ratio == lane_of((cols, LANES)),
        1.0 / (row_ratio * col_ratio),
        0.0,
    ).astype(BF16)
    rowc[1] = COURANT_LON / cos_center
    rowc[2] = COURANT_LAT / cos_center * coslat(place + 1.0)
    rowc[3] = COURANT_LAT / cos_center * coslat(place)
    expand_m[0], expand_m[1] = expanders(all_cols, cols, col_ratio)

    def send_mass(step, level):
        weighted = level * field[4, :rows, :cols] * wide(rowc[0, :rows], cols // LANES)
        summed = weighted.reshape(crows, row_ratio, cols).sum(axis=1)
        mass = exact_dot(summed, gather_m[...])
        lanes = lane_of((SUB, LANES))
        packed = mass[:SUB]
        for part in range(1, crows // SUB):
            moved = turn(mass[part * SUB : (part + 1) * SUB], 32 * part, 1)
            packed = jnp.where(lanes >= 32 * part, moved, packed)
        mslot[step, lat, lon] = packed
        if step == 0:
            pl.semaphore_wait(barrier, lon_n + lat_n - 2)
        lon_copies = []
        for off in sorted(range(1, lon_n), key=lambda off: -min(off, lon_n - off)):
            lon_copies.append(
                (
                    off,
                    send(
                        mslot.at[step, lat, lon], mslot.at[step, lat, lon],
                        mass_ss.at[step, off], mass_rs.at[step, off], (lat, lon_peer[off]),
                    ),
                )
            )
        return lon_copies, forward(step, 0)

    def forward(step, lon_off):
        slot = lax.rem(lon + lon_n - lon_off, lon_n)
        return [
            send(
                mslot.at[step, lat, slot], mslot.at[step, lat, slot],
                all_ss.at[step, off, lon_off], all_rs.at[step, off, lon_off],
                (lat_peer[off], lon),
            )
            for off in range(1, lat_n)
        ]

    def send_band(step, lon_copies):
        copies = []
        for lon_off, copy in reversed(lon_copies):
            copy.wait_recv()
            copies += forward(step, lon_off)
        return copies

    def band_of(step, band):
        lanes = lane_of((SUB, LANES))
        rows_of = []
        for part in range(crows // SUB):
            pieces = [jnp.zeros((SUB, LANES), F32) for _ in range(width // LANES)]
            for block in range(-(-width // ccols)):
                first = ccols * block
                slot = mslot[step, band, (block - 1) % lon_n]
                moved = turn(slot, first - 32 * part, 1)
                low, begin = first // LANES, first % LANES
                pieces[low] = jnp.where(lanes >= begin, moved, pieces[low])
                if begin + ccols > LANES and low + 1 < width // LANES:
                    pieces[low + 1] = moved
            rows_of.append(jnp.concatenate(pieces, 1))
        return rows_of

    def send_partials(step, copies):
        for copy in copies:
            copy.wait_recv()
        mass = jnp.concatenate([part for band in range(lat_n) for part in band_of(step, band)], 0)
        both = [mass, turn(mass, ccols // 2, 1)]
        if jpad > jrows:
            blank = jnp.zeros((jpad - jrows, width), F32)
            both = [both[0], blank, both[1], blank]
        high, low = halves(jnp.concatenate(both, 0))
        left = khi[...]
        product = (
            jnp.dot(left, high, preferred_element_type=F32)
            + jnp.dot(klo[...], high, preferred_element_type=F32)
            + jnp.dot(left, low, preferred_element_type=F32)
        )
        lags, shift = ccols // 2, 1
        product = product.reshape(lags, 32, width)
        while lags % 2 == 0:
            product = product.reshape(lags // 2, 2, 32, width)
            lags //= 2
            moved = turn(product[:, 1].reshape(lags * 32, width), shift, 1)
            product = product[:, 0] + moved.reshape(lags, 32, width)
            shift *= 2
        total = product[0]
        for lag in range(1, lags):
            total = total + turn(product[lag], shift * lag, 1)
        lanes = lane_of((SUB, LANES))
        sent = []
        for off in range(lon_n):
            packed = None
            for part in range(4):
                got = take(
                    total[part * SUB : (part + 1) * SUB], ccols * (off + 1) - 1, ccols + 2, 32 * part
                )
                packed = got if part == 0 else jnp.where(lanes >= 32 * part, got, packed)
            if off == 0:
                precv[step, 0] = packed
            else:
                psend[step, off] = packed
                sent.append(
                    send(
                        psend.at[step, off], precv.at[step, off],
                        part_ss.at[step, off], part_rs.at[step, off], (lat, lon_peer[off]),
                    )
                )
        return sent

    def loading_of(step, copies):
        for copy in copies:
            copy.wait_recv()
        total = precv[step, 0]
        for off in range(1, lon_n):
            total = total + precv[step, off]
        return jnp.concatenate([turn(total, -32 * part, 1) for part in range(4)], 0)

    def prepare(step, level, old_lon, old_lat):
        sub = sub_of((SUB, all_cols))
        for here in range(tiles):
            at = pl.ds(here * SUB, SUB)
            cells = level[at, :]
            after = level[pl.ds((here + 1) % tiles * SUB, SUB), :]
            rise_east = turn(cells, all_cols - 1, 1) - cells
            rise_north = turn(jnp.where(sub == 0, after, cells), SUB - 1, 0) - cells
            ahead[step, 0, at, :] = coef[1, at, :] * old_lon[at, :] - coef[0, at, :] * rise_east
            ahead[step, 1, at, :] = coef[3, at, :] * old_lat[at, :] - coef[2, at, :] * rise_north

    loads[0].wait()
    loads[1].wait()
    field[4, :rows, :cols] = wet_in[...].astype(F32)
    mass_copies, band_copies = send_mass(0, field[0, :rows, :cols])
    pending = [copy for _, copy in mass_copies]

    for copy in loads[2:5]:
        copy.wait()
    lanes = lane_of((rows, LANES))
    edges = jnp.zeros((rows, LANES), F32)
    for index in range(5):
        right = turn(field[index, :rows, cols - LANES : cols], 2 + 2 * index, 1)
        left = turn(field[index, :rows, :LANES], 16 + 2 * index, 1)
        edges = jnp.where(lanes // 2 == index, right, edges)
        edges = jnp.where(lanes // 2 == 8 + index, left, edges)
    square = lonh_send.shape[2]
    edges = jnp.concatenate([edges, jnp.zeros((square - rows, LANES), F32)], 0).T
    lonh_send[0] = edges[:16]
    lonh_send[1] = edges[16:32]
    lonh_copies = [
        send(lonh_send.at[0], lonh_recv.at[0], lonh_ss.at[0], lonh_rs.at[0], (lat, east)),
        send(lonh_send.at[1], lonh_recv.at[1], lonh_ss.at[1], lonh_rs.at[1], (lat, west)),
    ]
    pending += lonh_copies

    loads[5].wait()
    kh_copies = [
        send(kin.at[0], kin.at[crows], kh_ss.at[0], kh_rs.at[0], (south, lon)),
        send(kin.at[crows - 1], kin.at[crows + 1], kh_ss.at[1], kh_rs.at[1], (north, lon)),
    ]
    pending += kh_copies
    kt[...] = jnp.zeros(kt.shape, F32)

    half = ccols // 2

    def put(row):
        cells = kin[row]
        if jpad > jrows:
            cells = jnp.concatenate([cells, jnp.zeros((ccols, jpad - jrows), F32)], 1)
        for part in range(2):
            for chunk in range(jpad // LANES):
                piece = cells[part * half : (part + 1) * half, chunk * LANES : (chunk + 1) * LANES]
                kt[part * (jpad // LANES) + chunk, pl.ds(row, half, stride=32), :] = piece

    for row in range(crows):
        put(row)

    band_copies += send_band(0, mass_copies)
    pending += band_copies

    for copy in kh_copies:
        copy.wait_recv()
    put(crows)
    put(crows + 1)
    for chunk in range(kt.shape[0]):
        high, low = halves(kt[chunk])
        khi[:, chunk * LANES : (chunk + 1) * LANES] = high
        klo[:, chunk * LANES : (chunk + 1) * LANES] = low


    for copy in lonh_copies:
        copy.wait_recv()
    arrived = jnp.concatenate(
        [lonh_recv[0], lonh_recv[1], jnp.zeros((LANES - 32, square), F32)], 0
    ).T[:rows]
    for index in range(5):
        from_west = turn(arrived, LANES - 2 - 2 * index, 1)
        from_east = turn(arrived, -16 - 2 * index, 1)
        field[index, :rows, cols:] = jnp.where(lanes < LANES // 2, from_east, from_west)
    sub = sub_of((SUB, all_cols))
    for side in range(2):
        packs = [jnp.zeros((SUB, all_cols), F32), jnp.zeros((SUB, all_cols), F32)]
        for index in range(5):
            if side == 0:
                edge = turn(field[index, rows - SUB : rows, :], 2 + 2 * index, 0)
            else:
                edge = turn(field[index, :SUB, :], 2 * index, 0)
            packs[index // 4] = jnp.where(sub // 2 == index % 4, edge, packs[index // 4])
        lath_send[side] = jnp.concatenate(packs, 0)
    lath_copies = [
        send(lath_send.at[0], lath_recv.at[0], lath_ss.at[0], lath_rs.at[0], (north, lon)),
        send(lath_send.at[1], lath_recv.at[1], lath_ss.at[1], lath_rs.at[1], (south, lon)),
    ]
    pending += lath_copies

    part_copies = send_partials(0, band_copies)
    pending += part_copies

    for copy in lath_copies:
        copy.wait_recv()
    for index in range(5):
        part = pl.ds(SUB * (index // 4), SUB)
        from_south = turn(lath_recv[0, part, :], 6 - 2 * index, 0)
        from_north = turn(lath_recv[1, part, :], -2 * index, 0)
        if index == 4:
            from_south = jnp.where(lat == 0, 0.0, 1.0) * from_south
            from_north = jnp.where(lat == lat_n - 1, 0.0, 1.0) * from_north
        field[index, rows:, :] = jnp.where(sub < SUB // 2, from_north, from_south)

    for here in range(tiles):
        at = pl.ds(here * SUB, SUB)
        up_at = pl.ds((here + 1) % tiles * SUB, SUB)
        deep, sea = field[3, at, :], field[4, at, :]
        deep_north = turn(jnp.where(sub == 0, field[3, up_at, :], deep), SUB - 1, 0)
        sea_north = turn(jnp.where(sub == 0, field[4, up_at, :], sea), SUB - 1, 0)
        both = sea * turn(sea, all_cols - 1, 1)
        coef[1, at, :] = both
        coef[0, at, :] = (
            both
            * wide(rowc[1, at, :], all_cols // LANES)
            * (0.5 * (deep + turn(deep, all_cols - 1, 1)))
        )
        both = sea * sea_north
        coef[3, at, :] = both
        coef[2, at, :] = both * (COURANT_LAT * 0.5) * (deep + deep_north)
    prepare(0, field.at[0], field.at[1], field.at[2])

    results = []

    def keep(*pairs):
        for src, dst in pairs:
            copy = pltpu.make_async_copy(src, dst, out_sem.at[len(results)])
            copy.start()
            results.append(copy)

    keep(
        (rowc, out_rowc),
        (coef.at[0], out_pack.at[0]),
        (coef.at[2], out_pack.at[1]),
        (field.at[4], out_pack.at[2]),
    )
    rises = spread(loading_of(0, part_copies), crows, expand_m[0], expand_m[1])
    advance(
        field.at[0], (ahead.at[0, 0], ahead.at[0, 1]), (coef.at[0], coef.at[2]), field.at[4],
        rowc, rises, state, False, lambda tile: None, lambda tile: None,
    )

    mass_copies, band_copies = send_mass(1, state[0, :rows, :cols])
    prepare(1, state.at[0], state.at[1], state.at[2])
    keep(
        (ahead.at[1, 0], out_pack.at[3]),
        (ahead.at[1, 1], out_pack.at[4]),
        (state.at[0], out_pack.at[5]),
    )
    band_copies += send_band(1, mass_copies)
    part_copies = send_partials(1, band_copies)
    pending += [copy for _, copy in mass_copies] + band_copies + part_copies
    out_loading[...] = loading_of(1, part_copies)
    for copy in pending:
        copy.wait_send()
    for copy in results:
        copy.wait()


def body(height, flux_lon, flux_lat, depth, wet, kernel):
    lat_n, lon_n = lax.axis_size("lat"), lax.axis_size("lon")
    rows, cols = height.shape
    kernel = kernel.transpose(0, 2, 1)
    crows, ccols, jrows = kernel.shape
    all_rows, all_cols = rows + SUB, cols + LANES
    jpad = up(jrows, LANES)
    square = up(rows, LANES)
    lags = 32 * ccols // 2
    dma = pltpu.SemaphoreType.DMA
    block = jax.ShapeDtypeStruct((rows, cols), F32)
    inside = pl.BlockSpec(memory_space=pltpu.VMEM)
    pack = jax.ShapeDtypeStruct((6, all_rows, all_cols), F32)
    factors = jax.ShapeDtypeStruct((4, all_rows, LANES), F32)
    anywhere = pl.BlockSpec(memory_space=pl.ANY)
    results = pl.pallas_call(
        functools.partial(run, lat_n, lon_n),
        out_shape=[pack, factors, jax.ShapeDtypeStruct((32, LANES), F32)],
        in_specs=[anywhere] * 6,
        out_specs=[anywhere, anywhere, inside],
        scratch_shapes=[
            pltpu.VMEM((5, all_rows, all_cols), F32),
            pltpu.VMEM((rows, cols), jnp.int32),
            pltpu.VMEM((crows + 2, ccols, jrows), F32),
            pltpu.VMEM((3, all_rows, all_cols), F32),
            pltpu.VMEM((4, all_rows, all_cols), F32),
            pltpu.VMEM((4, all_rows, LANES), F32),
            pltpu.VMEM((STEPS, 2, all_rows, all_cols), F32),
            pltpu.VMEM((cols, LANES), BF16),
            pltpu.VMEM((2, LANES, all_cols), BF16),
            pltpu.VMEM((2 * jpad // LANES, lags, LANES), F32),
            pltpu.VMEM((lags, 2 * jpad), BF16),
            pltpu.VMEM((lags, 2 * jpad), BF16),
            pltpu.VMEM((STEPS, lat_n, lon_n, SUB, LANES), F32),
            pltpu.VMEM((STEPS, lon_n, SUB, LANES), F32),
            pltpu.VMEM((STEPS, lon_n, SUB, LANES), F32),
            pltpu.VMEM((2, 16, square), F32),
            pltpu.VMEM((2, 16, square), F32),
            pltpu.VMEM((2, 16, all_cols), F32),
            pltpu.VMEM((2, 16, all_cols), F32),
            dma((6,)),
            dma((7,)),
            dma((STEPS, lon_n)),
            dma((STEPS, lon_n)),
            dma((STEPS, lat_n, lon_n)),
            dma((STEPS, lat_n, lon_n)),
            dma((STEPS, lon_n)),
            dma((STEPS, lon_n)),
            dma((2,)),
            dma((2,)),
            dma((2,)),
            dma((2,)),
            dma((2,)),
            dma((2,)),
        ],
        compiler_params=pltpu.CompilerParams(
            collective_id=0, has_side_effects=True, vmem_limit_bytes=64 * 2**20
        ),
    )(height, flux_lon, flux_lat, depth, wet, kernel)
    return pl.pallas_call(
        finish,
        out_shape=[block, block, block, jax.ShapeDtypeStruct((crows, ccols), F32)],
        in_specs=[anywhere] * 3,
        out_specs=[anywhere] * 3 + [inside],
        scratch_shapes=[
            pltpu.VMEM((6, all_rows, all_cols), F32),
            pltpu.VMEM((4, all_rows, LANES), F32),
            pltpu.VMEM((32, LANES), F32),
            pltpu.VMEM((3, all_rows, all_cols), F32),
            dma((GROUPS + 1,)),
            dma(()),
            dma(()),
            dma((3, GROUPS)),
        ],
        compiler_params=pltpu.CompilerParams(vmem_limit_bytes=64 * 2**20),
    )(*results)


def solution(mesh):
    return jax.shard_map(
        body,
        mesh=mesh,
        in_specs=(P("lat", "lon"),) * 5 + (P("lat", None, "lon"),),
        out_specs=(P("lat", "lon"),) * 4,
        check_vma=False,
    )
```

```python
import functools
import math

import jax
import jax.numpy as jnp
from jax import lax
from jax.experimental import pallas as pl
from jax.experimental.pallas import tpu as pltpu
from jax.sharding import PartitionSpec as P

STEPS = 2
ANGLE_STEP = math.pi / (180.0 * 240.0)
COURANT_LON = 0.3
COURANT_LAT = 0.3
MESH = pl.DeviceIdType.MESH
LANES = 128
SUB = 8
F32 = jnp.float32
BF16 = jnp.bfloat16


def up(value, unit):
    return -(-value // unit) * unit


def lane_of(shape):
    return lax.broadcasted_iota(jnp.int32, shape, len(shape) - 1)


def sub_of(shape):
    return lax.broadcasted_iota(jnp.int32, shape, len(shape) - 2)


def turn(cells, shift, axis):
    shift = shift % cells.shape[axis]
    return cells if shift == 0 else pltpu.roll(cells, shift, axis)


def take(cells, start, width, dest):
    first, offset = start // LANES, start % LANES
    head = turn(cells[:, first * LANES : (first + 1) * LANES], dest - offset, 1)
    if offset + width <= LANES:
        return head
    tail = turn(cells[:, (first + 1) * LANES : (first + 2) * LANES], dest - offset, 1)
    return jnp.where(lane_of(head.shape) < dest + LANES - offset, head, tail)


def halves(cells):
    high = cells.astype(BF16)
    return high, (cells - high.astype(F32)).astype(BF16)


def exact_dot(cells, picks):
    high = cells.astype(BF16).astype(F32)
    rest = cells - high
    middle = rest.astype(BF16).astype(F32)
    terms = jnp.concatenate([high, middle, rest - middle], 0).astype(BF16)
    summed = jnp.dot(terms, picks, preferred_element_type=F32)
    rows = cells.shape[0]
    return summed[:rows] + (summed[rows : 2 * rows] + summed[2 * rows :])


def wide(cells, count):
    return jnp.concatenate([cells] * count, 1)


def expanders(all_cols, cols, col_ratio):
    shape = (LANES, all_cols)
    fine = lane_of(shape)

    def cell(column):
        coarse = jnp.where(column < cols + LANES // 2, 1 + column // col_ratio, 0)
        return jnp.where(sub_of(shape) == coarse, 1.0, 0.0)

    own = cell(fine)
    east = cell(jnp.where(fine == all_cols - 1, 0, fine + 1))
    return own.astype(BF16), (east - own).astype(BF16)


def spread(loading, crows, expand, expand_rise):
    following = turn(loading, loading.shape[0] - 1, 0)
    first = jnp.broadcast_to(loading[:1], loading.shape)
    north_rise = jnp.where(sub_of(loading.shape) < crows, following - loading, first - following)
    return exact_dot(loading, expand_rise), exact_dot(north_rise, expand)


def advance(level, ahead, factor, sea, rowc, rises, new, last, before, after):
    all_rows, all_cols = level.shape
    tiles = all_rows // SUB
    sub = sub_of((SUB, all_cols))
    east_rise, north_rise = rises
    count = all_cols // LANES

    def lat_of(tile):
        at = pl.ds(tile * SUB, SUB)
        rise = jnp.broadcast_to(north_rise[tile : tile + 1], (SUB, all_cols))
        return ahead[1][at, :] - factor[1][at, :] * jnp.where(sub == SUB - 1, rise, 0.0)

    before(tiles - 1)
    below = lat_of(tiles - 1)
    for tile in range(tiles - 1 if last else tiles):
        before(tile)
        at = pl.ds(tile * SUB, SUB)
        rise = jnp.broadcast_to(east_rise[tile : tile + 1], (SUB, all_cols))
        if tile == tiles - 1:
            south_rise = jnp.broadcast_to(east_rise[tile + 1 : tile + 2], (SUB, all_cols))
            rise = jnp.where(sub < SUB // 2, rise, south_rise)
        lon_new = ahead[0][at, :] - factor[0][at, :] * rise
        lat_new = lat_of(tile)
        lat_south = turn(jnp.where(sub == SUB - 1, below, lat_new), 1, 0)
        below = lat_new
        new[1, at, :] = lon_new
        new[2, at, :] = lat_new
        new[0, at, :] = sea[at, :] * (
            level[at, :]
            - wide(rowc[1, at, :], count) * (lon_new - turn(lon_new, 1, 1))
            - (
                wide(rowc[2, at, :], count) * lat_new
                - wide(rowc[3, at, :], count) * lat_south
            )
        )
        after(tile)


GROUPS = 3


def finish(
    pack, rowc_in, loading_in, out_height, out_lon, out_lat, out_loading,
    have, rowc, loading_ref, final, pack_sem, row_sem, load_sem, out_sem,
):
    rows, cols = out_height.shape
    crows, ccols = out_loading.shape
    all_rows, all_cols = have.shape[1:]
    tiles = all_rows // SUB
    group = rows // GROUPS
    get_loading = pltpu.make_async_copy(loading_in, loading_ref, load_sem)
    get_rowc = pltpu.make_async_copy(rowc_in, rowc, row_sem)
    parts = [pl.ds(rows, SUB)] + [pl.ds(index * group, group) for index in range(GROUPS)]
    gets = [
        pltpu.make_async_copy(pack.at[:, part], have.at[:, part], pack_sem.at[index])
        for index, part in enumerate(parts)
    ]
    for copy in [get_loading, get_rowc, *gets]:
        copy.start()
    expand, expand_rise = expanders(all_cols, cols, cols // ccols)
    get_loading.wait()
    loading = loading_ref[...]
    out_loading[...] = turn(loading[:crows], -1, 1)[:, :ccols]
    rises = spread(loading, crows, expand, expand_rise)
    get_rowc.wait()
    puts = []
    per = group // SUB

    def before(tile):
        if tile == tiles - 1:
            gets[0].wait()
        elif tile % per == 0:
            gets[1 + tile // per].wait()

    def after(tile):
        if tile % per == per - 1:
            part = parts[1 + tile // per]
            for index, out in enumerate((out_height, out_lon, out_lat)):
                copy = pltpu.make_async_copy(
                    final.at[index, part, pl.ds(0, cols)],
                    out.at[part],
                    out_sem.at[index, tile // per],
                )
                copy.start()
                puts.append(copy)

    advance(
        have.at[5], (have.at[3], have.at[4]), (have.at[0], have.at[1]), have.at[2], rowc, rises,
        final, True, before, after,
    )
    for copy in puts:
        copy.wait()


def run(
    lat_n, lon_n,
    height, flux_lon, flux_lat, depth, wet, kernel,
    out_pack, out_rowc, out_loading,
    field, wet_in, kin, state, coef, rowc, ahead, gather_m, expand_m,
    kt, khi, klo, mslot, mass_all, psend, precv,
    lonh_send, lonh_recv, lath_send, lath_recv,
    in_sem, out_sem, mass_ss, mass_rs, all_ss, all_rs, part_ss, part_rs,
    kh_ss, kh_rs, lonh_ss, lonh_rs, lath_ss, lath_rs,
):
    lat, lon = lax.axis_index("lat"), lax.axis_index("lon")
    rows, cols = height.shape
    crows, ccols, jrows = kernel.shape
    all_rows, all_cols = field.shape[1:]
    tiles = all_rows // SUB
    jpad = up(jrows, LANES)
    width = mass_all.shape[2]
    north, south = lax.rem(lat + 1, lat_n), lax.rem(lat + lat_n - 1, lat_n)
    east, west = lax.rem(lon + 1, lon_n), lax.rem(lon + lon_n - 1, lon_n)
    lon_peer = [lax.rem(lon + off, lon_n) for off in range(lon_n)]
    lat_peer = [lax.rem(lat + off, lat_n) for off in range(lat_n)]

    def send(src, dst, ss, rs, to):
        copy = pltpu.make_async_remote_copy(
            src_ref=src, dst_ref=dst, send_sem=ss, recv_sem=rs, device_id=to, device_id_type=MESH
        )
        copy.start()
        return copy

    own = (pl.ds(0, rows), pl.ds(0, cols))
    loads = [
        pltpu.make_async_copy(height, field.at[(0, *own)], in_sem.at[0]),
        pltpu.make_async_copy(wet, wet_in, in_sem.at[4]),
        pltpu.make_async_copy(flux_lon, field.at[(1, *own)], in_sem.at[1]),
        pltpu.make_async_copy(flux_lat, field.at[(2, *own)], in_sem.at[2]),
        pltpu.make_async_copy(depth, field.at[(3, *own)], in_sem.at[3]),
        pltpu.make_async_copy(kernel, kin.at[pl.ds(0, crows)], in_sem.at[5]),
    ]
    for copy in loads:
        copy.start()
    barrier = pltpu.get_barrier_semaphore()
    for off in range(1, lon_n):
        pl.semaphore_signal(barrier, inc=1, device_id=(lat, lon_peer[off]), device_id_type=MESH)
    for off in range(1, lat_n):
        pl.semaphore_signal(barrier, inc=1, device_id=(lat_peer[off], lon), device_id_type=MESH)

    place = sub_of((all_rows, LANES))
    place = jnp.where(place >= all_rows - SUB // 2, place - all_rows, place) + lat * rows
    place = place.astype(F32)

    def coslat(position):
        return jnp.cos((position - 0.5 * (rows * lat_n)) * ANGLE_STEP)

    cos_center = coslat(place + 0.5)
    rowc[0] = cos_center
    row_ratio, col_ratio = rows // crows, cols // ccols
    gather_m[...] = jnp.where(
        lax.broadcasted_iota(jnp.int32, (cols, LANES), 0) // col_ratio == lane_of((cols, LANES)),
        1.0 / (row_ratio * col_ratio),
        0.0,
    ).astype(BF16)
    rowc[1] = COURANT_LON / cos_center
    rowc[2] = COURANT_LAT / cos_center * coslat(place + 1.0)
    rowc[3] = COURANT_LAT / cos_center * coslat(place)
    expand_m[0], expand_m[1] = expanders(all_cols, cols, col_ratio)

    def send_mass(step, level):
        weighted = level * field[4, :rows, :cols] * wide(rowc[0, :rows], cols // LANES)
        summed = weighted.reshape(crows, row_ratio, cols).sum(axis=1)
        mass = exact_dot(summed, gather_m[...])
        lanes = lane_of((SUB, LANES))
        packed = mass[:SUB]
        for part in range(1, crows // SUB):
            moved = turn(mass[part * SUB : (part + 1) * SUB], 32 * part, 1)
            packed = jnp.where(lanes >= 32 * part, moved, packed)
        mslot[step, lon] = packed
        if step == 0:
            pl.semaphore_wait(barrier, lon_n + lat_n - 2)
        return [
            send(
                mslot.at[step, lon], mslot.at[step, lon],
                mass_ss.at[step, off], mass_rs.at[step, off], (lat, lon_peer[off]),
            )
            for off in range(1, lon_n)
        ]

    def send_band(step, copies):
        for copy in copies:
            copy.wait_recv()
        lanes = lane_of((SUB, LANES))
        bands = []
        for part in range(crows // SUB):
            pieces = [jnp.zeros((SUB, LANES), F32) for _ in range(width // LANES)]
            for block in range(-(-width // ccols)):
                first = ccols * block
                slot = mslot[step, (block - 1) % lon_n]
                moved = turn(slot, first - 32 * part, 1)
                low, begin = first // LANES, first % LANES
                pieces[low] = jnp.where(lanes >= begin, moved, pieces[low])
                if begin + ccols > LANES and low + 1 < width // LANES:
                    pieces[low + 1] = moved
            bands.append(jnp.concatenate(pieces, 1))
        here = pl.ds(pl.multiple_of(lat * crows, SUB), crows)
        mass_all[step, here] = jnp.concatenate(bands, 0)
        return [
            send(
                mass_all.at[step, here], mass_all.at[step, here],
                all_ss.at[step, off], all_rs.at[step, off], (lat_peer[off], lon),
            )
            for off in range(1, lat_n)
        ]

    def send_partials(step, copies):
        for copy in copies:
            copy.wait_recv()
        mass = mass_all[step]
        both = [mass, turn(mass, ccols // 2, 1)]
        if jpad > jrows:
            blank = jnp.zeros((jpad - jrows, width), F32)
            both = [both[0], blank, both[1], blank]
        high, low = halves(jnp.concatenate(both, 0))
        left = khi[...]
        product = (
            jnp.dot(left, high, preferred_element_type=F32)
            + jnp.dot(klo[...], high, preferred_element_type=F32)
            + jnp.dot(left, low, preferred_element_type=F32)
        )
        lags, shift = ccols // 2, 1
        product = product.reshape(lags, 32, width)
        while lags % 2 == 0:
            product = product.reshape(lags // 2, 2, 32, width)
            lags //= 2
            moved = turn(product[:, 1].reshape(lags * 32, width), shift, 1)
            product = product[:, 0] + moved.reshape(lags, 32, width)
            shift *= 2
        total = product[0]
        for lag in range(1, lags):
            total = total + turn(product[lag], shift * lag, 1)
        lanes = lane_of((SUB, LANES))
        sent = []
        for off in range(lon_n):
            packed = None
            for part in range(4):
                got = take(
                    total[part * SUB : (part + 1) * SUB], ccols * (off + 1) - 1, ccols + 2, 32 * part
                )
                packed = got if part == 0 else jnp.where(lanes >= 32 * part, got, packed)
            if off == 0:
                precv[step, 0] = packed
            else:
                psend[step, off] = packed
                sent.append(
                    send(
                        psend.at[step, off], precv.at[step, off],
                        part_ss.at[step, off], part_rs.at[step, off], (lat, lon_peer[off]),
                    )
                )
        return sent

    def loading_of(step, copies):
        for copy in copies:
            copy.wait_recv()
        total = precv[step, 0]
        for off in range(1, lon_n):
            total = total + precv[step, off]
        return jnp.concatenate([turn(total, -32 * part, 1) for part in range(4)], 0)

    def factors(which):
        sub = sub_of((SUB, all_cols))
        for here in which:
            at = pl.ds(here * SUB, SUB)
            up_at = pl.ds((here + 1) % tiles * SUB, SUB)
            deep, sea = field[3, at, :], field[4, at, :]
            deep_north = turn(jnp.where(sub == 0, field[3, up_at, :], deep), SUB - 1, 0)
            sea_north = turn(jnp.where(sub == 0, field[4, up_at, :], sea), SUB - 1, 0)
            both = sea * turn(sea, all_cols - 1, 1)
            coef[1, at, :] = both
            coef[0, at, :] = (
                both
                * wide(rowc[1, at, :], all_cols // LANES)
                * (0.5 * (deep + turn(deep, all_cols - 1, 1)))
            )
            both = sea * sea_north
            coef[3, at, :] = both
            coef[2, at, :] = both * (COURANT_LAT * 0.5) * (deep + deep_north)

    def prepare(step, level, old_lon, old_lat, which):
        sub = sub_of((SUB, all_cols))
        for here in which:
            at = pl.ds(here * SUB, SUB)
            cells = level[at, :]
            after = level[pl.ds((here + 1) % tiles * SUB, SUB), :]
            rise_east = turn(cells, all_cols - 1, 1) - cells
            rise_north = turn(jnp.where(sub == 0, after, cells), SUB - 1, 0) - cells
            ahead[step, 0, at, :] = coef[1, at, :] * old_lon[at, :] - coef[0, at, :] * rise_east
            ahead[step, 1, at, :] = coef[3, at, :] * old_lat[at, :] - coef[2, at, :] * rise_north

    loads[0].wait()
    loads[1].wait()
    field[4, :rows, :cols] = wet_in[...].astype(F32)
    mass_copies = send_mass(0, field[0, :rows, :cols])
    pending = list(mass_copies)

    for copy in loads[2:5]:
        copy.wait()
    lanes = lane_of((rows, LANES))
    edges = jnp.zeros((rows, LANES), F32)
    for index in range(5):
        right = turn(field[index, :rows, cols - LANES : cols], 2 + 2 * index, 1)
        left = turn(field[index, :rows, :LANES], 16 + 2 * index, 1)
        edges = jnp.where(lanes // 2 == index, right, edges)
        edges = jnp.where(lanes // 2 == 8 + index, left, edges)
    square = lonh_send.shape[2]
    edges = jnp.concatenate([edges, jnp.zeros((square - rows, LANES), F32)], 0).T
    lonh_send[0] = edges[:16]
    lonh_send[1] = edges[16:32]
    lonh_copies = [
        send(lonh_send.at[0], lonh_recv.at[0], lonh_ss.at[0], lonh_rs.at[0], (lat, east)),
        send(lonh_send.at[1], lonh_recv.at[1], lonh_ss.at[1], lonh_rs.at[1], (lat, west)),
    ]
    pending += lonh_copies

    loads[5].wait()
    kh_copies = [
        send(kin.at[0], kin.at[crows], kh_ss.at[0], kh_rs.at[0], (south, lon)),
        send(kin.at[crows - 1], kin.at[crows + 1], kh_ss.at[1], kh_rs.at[1], (north, lon)),
    ]
    pending += kh_copies
    kt[...] = jnp.zeros(kt.shape, F32)

    half = ccols // 2

    def put(row):
        cells = kin[row]
        if jpad > jrows:
            cells = jnp.concatenate([cells, jnp.zeros((ccols, jpad - jrows), F32)], 1)
        for part in range(2):
            for chunk in range(jpad // LANES):
                piece = cells[part * half : (part + 1) * half, chunk * LANES : (chunk + 1) * LANES]
                kt[part * (jpad // LANES) + chunk, pl.ds(row, half, stride=32), :] = piece

    for row in range(crows):
        put(row)

    band_copies = send_band(0, mass_copies)
    pending += band_copies

    for copy in kh_copies:
        copy.wait_recv()
    put(crows)
    put(crows + 1)
    for chunk in range(kt.shape[0]):
        high, low = halves(kt[chunk])
        khi[:, chunk * LANES : (chunk + 1) * LANES] = high
        klo[:, chunk * LANES : (chunk + 1) * LANES] = low


    for copy in lonh_copies:
        copy.wait_recv()
    arrived = jnp.concatenate(
        [lonh_recv[0], lonh_recv[1], jnp.zeros((LANES - 32, square), F32)], 0
    ).T[:rows]
    for index in range(5):
        from_west = turn(arrived, LANES - 2 - 2 * index, 1)
        from_east = turn(arrived, -16 - 2 * index, 1)
        field[index, :rows, cols:] = jnp.where(lanes < LANES // 2, from_east, from_west)
    sub = sub_of((SUB, all_cols))
    for side in range(2):
        packs = [jnp.zeros((SUB, all_cols), F32), jnp.zeros((SUB, all_cols), F32)]
        for index in range(5):
            if side == 0:
                edge = turn(field[index, rows - SUB : rows, :], 2 + 2 * index, 0)
            else:
                edge = turn(field[index, :SUB, :], 2 * index, 0)
            packs[index // 4] = jnp.where(sub // 2 == index % 4, edge, packs[index // 4])
        lath_send[side] = jnp.concatenate(packs, 0)
    lath_copies = [
        send(lath_send.at[0], lath_recv.at[0], lath_ss.at[0], lath_rs.at[0], (north, lon)),
        send(lath_send.at[1], lath_recv.at[1], lath_ss.at[1], lath_rs.at[1], (south, lon)),
    ]
    pending += lath_copies

    part_copies = send_partials(0, band_copies)
    pending += part_copies

    factors(range(tiles - 2))
    prepare(0, field.at[0], field.at[1], field.at[2], range(tiles - 2))
    for copy in lath_copies:
        copy.wait_recv()
    for index in range(5):
        part = pl.ds(SUB * (index // 4), SUB)
        from_south = turn(lath_recv[0, part, :], 6 - 2 * index, 0)
        from_north = turn(lath_recv[1, part, :], -2 * index, 0)
        if index == 4:
            from_south = jnp.where(lat == 0, 0.0, 1.0) * from_south
            from_north = jnp.where(lat == lat_n - 1, 0.0, 1.0) * from_north
        field[index, rows:, :] = jnp.where(sub < SUB // 2, from_north, from_south)

    factors(range(tiles - 2, tiles))
    prepare(0, field.at[0], field.at[1], field.at[2], range(tiles - 2, tiles))

    results = []

    def keep(*pairs):
        for src, dst in pairs:
            copy = pltpu.make_async_copy(src, dst, out_sem.at[len(results)])
            copy.start()
            results.append(copy)

    keep(
        (rowc, out_rowc),
        (coef.at[0], out_pack.at[0]),
        (coef.at[2], out_pack.at[1]),
        (field.at[4], out_pack.at[2]),
    )
    rises = spread(loading_of(0, part_copies), crows, expand_m[0], expand_m[1])
    advance(
        field.at[0], (ahead.at[0, 0], ahead.at[0, 1]), (coef.at[0], coef.at[2]), field.at[4],
        rowc, rises, state, False, lambda tile: None, lambda tile: None,
    )

    mass_copies = send_mass(1, state[0, :rows, :cols])
    prepare(1, state.at[0], state.at[1], state.at[2], range(tiles))
    keep(
        (ahead.at[1, 0], out_pack.at[3]),
        (ahead.at[1, 1], out_pack.at[4]),
        (state.at[0], out_pack.at[5]),
    )
    band_copies = send_band(1, mass_copies)
    part_copies = send_partials(1, band_copies)
    pending += mass_copies + band_copies + part_copies
    out_loading[...] = loading_of(1, part_copies)
    for copy in pending:
        copy.wait_send()
    for copy in results:
        copy.wait()


def body(height, flux_lon, flux_lat, depth, wet, kernel):
    lat_n, lon_n = lax.axis_size("lat"), lax.axis_size("lon")
    rows, cols = height.shape
    kernel = kernel.transpose(0, 2, 1)
    crows, ccols, jrows = kernel.shape
    all_rows, all_cols = rows + SUB, cols + LANES
    jpad = up(jrows, LANES)
    width = up(ccols * lon_n + ccols + 1, LANES)
    square = up(rows, LANES)
    lags = 32 * ccols // 2
    dma = pltpu.SemaphoreType.DMA
    block = jax.ShapeDtypeStruct((rows, cols), F32)
    inside = pl.BlockSpec(memory_space=pltpu.VMEM)
    pack = jax.ShapeDtypeStruct((6, all_rows, all_cols), F32)
    factors = jax.ShapeDtypeStruct((4, all_rows, LANES), F32)
    anywhere = pl.BlockSpec(memory_space=pl.ANY)
    results = pl.pallas_call(
        functools.partial(run, lat_n, lon_n),
        out_shape=[pack, factors, jax.ShapeDtypeStruct((32, LANES), F32)],
        in_specs=[anywhere] * 6,
        out_specs=[anywhere, anywhere, inside],
        scratch_shapes=[
            pltpu.VMEM((5, all_rows, all_cols), F32),
            pltpu.VMEM((rows, cols), jnp.int32),
            pltpu.VMEM((crows + 2, ccols, jrows), F32),
            pltpu.VMEM((3, all_rows, all_cols), F32),
            pltpu.VMEM((4, all_rows, all_cols), F32),
            pltpu.VMEM((4, all_rows, LANES), F32),
            pltpu.VMEM((STEPS, 2, all_rows, all_cols), F32),
            pltpu.VMEM((cols, LANES), BF16),
            pltpu.VMEM((2, LANES, all_cols), BF16),
            pltpu.VMEM((2 * jpad // LANES, lags, LANES), F32),
            pltpu.VMEM((lags, 2 * jpad), BF16),
            pltpu.VMEM((lags, 2 * jpad), BF16),
            pltpu.VMEM((STEPS, lon_n, SUB, LANES), F32),
            pltpu.VMEM((STEPS, jrows, width), F32),
            pltpu.VMEM((STEPS, lon_n, SUB, LANES), F32),
            pltpu.VMEM((STEPS, lon_n, SUB, LANES), F32),
            pltpu.VMEM((2, 16, square), F32),
            pltpu.VMEM((2, 16, square), F32),
            pltpu.VMEM((2, 16, all_cols), F32),
            pltpu.VMEM((2, 16, all_cols), F32),
            dma((6,)),
            dma((7,)),
            dma((STEPS, lon_n)),
            dma((STEPS, lon_n)),
            dma((STEPS, lat_n)),
            dma((STEPS, lat_n)),
            dma((STEPS, lon_n)),
            dma((STEPS, lon_n)),
            dma((2,)),
            dma((2,)),
            dma((2,)),
            dma((2,)),
            dma((2,)),
            dma((2,)),
        ],
        compiler_params=pltpu.CompilerParams(
            collective_id=0, has_side_effects=True, vmem_limit_bytes=64 * 2**20
        ),
    )(height, flux_lon, flux_lat, depth, wet, kernel)
    return pl.pallas_call(
        finish,
        out_shape=[block, block, block, jax.ShapeDtypeStruct((crows, ccols), F32)],
        in_specs=[anywhere] * 3,
        out_specs=[anywhere] * 3 + [inside],
        scratch_shapes=[
            pltpu.VMEM((6, all_rows, all_cols), F32),
            pltpu.VMEM((4, all_rows, LANES), F32),
            pltpu.VMEM((32, LANES), F32),
            pltpu.VMEM((3, all_rows, all_cols), F32),
            dma((GROUPS + 1,)),
            dma(()),
            dma(()),
            dma((3, GROUPS)),
        ],
        compiler_params=pltpu.CompilerParams(vmem_limit_bytes=64 * 2**20),
    )(*results)


def solution(mesh):
    return jax.shard_map(
        body,
        mesh=mesh,
        in_specs=(P("lat", "lon"),) * 5 + (P("lat", None, "lon"),),
        out_specs=(P("lat", "lon"),) * 4,
        check_vma=False,
    )
```
